768 devices in a mesh: row: 16 (over y, core), col: 4 (over x), depth: 12 (over z).
Axes of the slice: x: 4, y: 8, z: 12, core: 2. Of those that a mesh axis runs over, the one named last changes fastest.
Arguments:
- row_stripe: bfloat16 [1920, 12, 8704], P('row', 'depth', 'col'), may hold values from -0.01953125 to 0.01953125
- column_stripe: bfloat16 [12, 8704, 1920], P('depth', 'row', 'col'), may hold values from -9 to 9
- window_block: bfloat16 [1920, 1920], P('row', ('col', 'depth')), may hold values from -3 to 3
- stripe_tiles: int32 [15, 816], replicated, may hold values 0 or 1
- column_tiles: int32 [816, 15], replicated, may hold values 0 or 1
- keep_tiles: int32 [15, 15], replicated, may hold values 0 or 1
- branch: int32 [15], replicated, may hold values from 0 to 1
Outputs:
- new_block: bfloat16 [1920, 1920], P('row', ('col', 'depth'))
- occupancy: float32 [], replicated
The draws below stay inside these ranges and needn't reach their ends.
All inputs are finite; a program needn't handle non-finite values.
Results may differ from the reference program's by a relative error of at most 0.0018.
Values may be sent and summed in bfloat16 or wider, within the bound.
A program may use at most 32 MiB of HBM per device.

```python
import jax
import jax.numpy as jnp
from jax import lax

ORDER = 104448
TILE = 128
WIN = 1920
LAYER = 8704
N_DEPTH = 12


def touch_ends(array, rng, smallest, high):
    extent = array.shape
    spot = [jax.random.randint(jax.random.fold_in(rng, axis), (), 0, extent[axis]) for axis in range(len(extent))]
    array = array.at[tuple(spot)].set(smallest)
    longest = extent.index(max(extent))
    spot[longest] = (spot[longest] + 1) % extent[longest]
    return array.at[tuple(spot)].set(high)


def steps_of(stream_key, extent, split, smallest, largest):
    def one(dim, shards_of):
        heights = jax.random.uniform(jax.random.fold_in(jax.random.fold_in(stream_key, 6), dim), (shards_of,), jnp.float32, smallest / len(split), largest / len(split))
        return jnp.repeat(jnp.exp(heights), extent[dim] // shards_of).reshape((-1,) + (1,) * (len(extent) - dim - 1))

    loudness = one(*split[0])
    for cut in split[1:]:
        loudness = loudness * one(*cut)
    return loudness


def centred(own_key, extent, spread, most, pieces=(), kind=jnp.bfloat16):
    drawn = spread * jax.random.normal(own_key, extent, jnp.float32)
    if pieces:
        drawn = drawn * steps_of(own_key, extent, pieces, -0.22, 0.18)
    return jnp.clip(drawn, -most, most).astype(kind)


def setup_inputs(seed: int = 0) -> dict:
    arg_keys = jax.random.split(jax.random.key(seed), 8)
    return {
        "row_stripe": centred(arg_keys[0], (WIN, N_DEPTH, LAYER), ORDER ** -0.5, 0.01953125, ((0, 16), (1, 12), (2, 4))),
        "column_stripe": centred(arg_keys[1], (N_DEPTH, LAYER, WIN), 1.5, 9.0, ((0, 12), (1, 16), (2, 4))),
        "window_block": centred(arg_keys[2], (WIN, WIN), 0.5, 3.0, ((0, 16), (1, 48))),
        "stripe_tiles": touch_ends((jax.random.randint(arg_keys[3], ((WIN + TILE - 1) // TILE, (ORDER + TILE - 1) // TILE), 0, 3) < 2).astype(jnp.int32), jax.random.fold_in(arg_keys[3], 1), 0, 1),
        "column_tiles": touch_ends((jax.random.randint(arg_keys[4], ((ORDER + TILE - 1) // TILE, (WIN + TILE - 1) // TILE), 0, 3) < 2).astype(jnp.int32), jax.random.fold_in(arg_keys[4], 1), 0, 1),
        "keep_tiles": touch_ends((jax.random.randint(arg_keys[5], ((WIN + TILE - 1) // TILE, (WIN + TILE - 1) // TILE), 0, 4) < 3).astype(jnp.int32), jax.random.fold_in(arg_keys[5], 1), 0, 1),
        "branch": touch_ends(jax.random.randint(arg_keys[6], ((WIN + TILE - 1) // TILE,), 0, 2), jax.random.fold_in(arg_keys[6], 1), 0, 1).astype(jnp.int32),
    }


def tile_mask(table, rows_wanted, cols_wanted):
    grown = jnp.repeat(jnp.repeat(table > 0, TILE, axis=0), TILE, axis=1)
    return grown[:rows_wanted, :cols_wanted]


def reference(row_stripe, column_stripe, window_block, stripe_tiles, column_tiles, keep_tiles, branch):
    left_rows = row_stripe.reshape(WIN, ORDER)
    left_rows = jnp.where(tile_mask(stripe_tiles, WIN, ORDER), left_rows, jnp.zeros((), jnp.bfloat16)).astype(jnp.float32)
    right_cols = column_stripe.reshape(ORDER, WIN)
    right_cols = jnp.where(tile_mask(column_tiles, ORDER, WIN), right_cols, jnp.zeros((), jnp.bfloat16)).astype(jnp.float32)
    occupancy = jnp.sum(left_rows * left_rows) / WIN
    square = jnp.dot(left_rows, right_cols, preferred_element_type=jnp.float32, precision=lax.Precision.HIGHEST)
    doubled = 2.0 * window_block.astype(jnp.float32) - square
    branch_rows = tile_mask(branch[:, None], WIN, 1)
    updated = jnp.where(branch_rows, doubled, square)
    new_block = jnp.where(tile_mask(keep_tiles, WIN, WIN), updated, jnp.zeros((), jnp.float32)).astype(jnp.bfloat16)
    return new_block, occupancy
```

```python
import functools

import jax
import jax.numpy as jnp
from jax import lax
from jax.experimental import pallas as pl
from jax.experimental.pallas import tpu as pltpu
from jax.sharding import PartitionSpec as P

TILE = 128
MESH = pl.DeviceIdType.MESH
X, Y, Z = 4, 8, 12
ROWS = 120
ROWS_P = 128
PANEL = 2176
SUB = 544
COLS = 480
OUT = 40
KWIN = 1152
EARLY = 1


def segments(tile):
    found = []
    for z in range(Z):
        low = max(tile * TILE, z * OUT)
        high = min(tile * TILE + TILE, COLS, z * OUT + OUT)
        if low < high:
            found.append((z, low - tile * TILE, high - low, low - z * OUT))
    return found


def one_hot(hit):
    return jnp.where(hit, 1.0, 0.0).astype(jnp.bfloat16)


def dot(a, b):
    return jnp.dot(a, b, preferred_element_type=jnp.float32)


def kernel(
    row_ref, col_ref, win_ref, stripe_ref, ctab_ref, keep_ref, branch_ref,
    out_ref, occ_ref,
    rm, rb, lg, acc, ct, zin, occx, occy, occc, occz, keepm, branchm,
    rsend, rrecv, dsend, drecv, own_sem, lsend, lrecv, lsibs, lsibr, zsend, zrecv, osend, orecv,
):
    r = lax.axis_index("row")
    x = lax.axis_index("col")
    z = lax.axis_index("depth")
    y = r // 2
    c = r % 2

    def ydev(d):
        return (((y + d) % Y) * 2 + c, x, z)

    def xdev(d):
        return (r, (x + d) % X, z)

    sib = (y * 2 + (1 - c), x, z)

    barrier = pltpu.get_barrier_semaphore()
    peers = [ydev(d) for d in range(1, Y)] + [xdev(d) for d in range(1, X)] + [sib]
    for d in range(1, Z):
        peers.append((r, x, (z + d) % Z))
        peers.append((y * 2 + (1 - c), x, (z + d) % Z))
    for peer in peers:
        pl.semaphore_signal(barrier, inc=1, device_id=peer, device_id_type=MESH)

    for t in range(2):
        for yy in range(Y):
            low = 0 if yy % 2 else 2 * SUB
            rb[t, yy, low : low + 64, :] = jnp.zeros((64, TILE), jnp.bfloat16)

    first = z * 68 + (r * SUB) // TILE
    skew = (r * SUB) % TILE
    ctab = one_hot(ctab_ref[...] > 0)
    pick = one_hot(
        lax.broadcasted_iota(jnp.int32, (16, 816), 1)
        == lax.broadcasted_iota(jnp.int32, (16, 816), 0) + first
    )
    picked = dot(pick, ctab).astype(jnp.bfloat16)
    spread = one_hot(
        lax.broadcasted_iota(jnp.int32, (15, 512), 0)
        == (lax.broadcasted_iota(jnp.int32, (15, 512), 1) + x * COLS) // TILE
    )
    by_col = dot(picked, spread).astype(jnp.bfloat16)
    band = one_hot(
        lax.broadcasted_iota(jnp.int32, (SUB, 16), 1)
        == (lax.broadcasted_iota(jnp.int32, (SUB, 16), 0) + skew) // TILE
    )
    rm[3] = jnp.zeros((SUB, TILE), jnp.bfloat16)
    for tile in range(4):
        wide = min(TILE, COLS - tile * TILE)
        mask = dot(band, by_col[:, tile * TILE : tile * TILE + wide]).astype(jnp.bfloat16)
        rm[tile, :, 0:wide] = col_ref[0, :, tile * TILE : tile * TILE + wide] * mask

    pl.semaphore_wait(barrier, len(peers))

    def off(yy, cc):
        return pl.multiple_of((yy % 2) * 64 + cc * SUB, 32)

    def piece(t, yy, cc):
        return rb.at[t, yy, pl.ds(off(yy, cc), SUB), :]

    def which(d, k):
        if k == 6:
            return c if d > 0 else 1 - c
        return c if k % 2 == 0 else 1 - c

    def sent(d, t, k):
        yy = (y - d * (k // 2) + Y) % Y
        there = piece(t, yy, which(d, k))
        here = rm.at[2 * c + t] if k == 0 else there
        i = (0 if d > 0 else 14) + t * 7 + k
        return pltpu.make_async_remote_copy(
            src_ref=here, dst_ref=there, send_sem=rsend.at[i], recv_sem=rrecv.at[i],
            device_id=ydev(d % Y), device_id_type=MESH,
        )

    def got(d, t, k):
        yy = (y - d * (k // 2 + 1) + Y) % Y
        here = piece(t, yy, which(d, k))
        i = (0 if d > 0 else 14) + t * 7 + k
        return pltpu.make_async_copy(here, here, rrecv.at[i])

    ways = (1, -1)
    for d in ways:
        sent(d, 0, 0).start()

    def swap(t):
        return pltpu.make_async_remote_copy(
            src_ref=rm.at[2 * (1 - c) + t], dst_ref=piece(t, y, c),
            send_sem=dsend.at[t], recv_sem=drecv.at[t], device_id=sib, device_id_type=MESH,
        )

    def keep_own(t):
        return pltpu.make_async_copy(rm.at[2 * c + t], piece(t, y, c), own_sem.at[t])

    def swapped(t):
        here = piece(t, y, 1 - c)
        return pltpu.make_async_copy(here, here, drecv.at[t])

    for t in range(2):
        swap(t).start()
        keep_own(t).start()

    stab = one_hot(stripe_ref[...] > 0)
    base = z * 68 + x * 17
    shift = one_hot(
        lax.broadcasted_iota(jnp.int32, (816, TILE), 0)
        == lax.broadcasted_iota(jnp.int32, (816, TILE), 1) + base
    )
    narrow = dot(stab, shift).astype(jnp.bfloat16)
    rows_in = one_hot(
        lax.broadcasted_iota(jnp.int32, (ROWS, 15), 1)
        == (lax.broadcasted_iota(jnp.int32, (ROWS, 15), 0) + r * ROWS) // TILE
    )
    lmask = dot(rows_in, narrow)
    total = jnp.zeros((8, TILE), jnp.float32)
    myrow = pl.multiple_of(c * ROWS_P, ROWS_P)
    for k in range(17):
        part = row_ref[:, 0, k * TILE : k * TILE + TILE].astype(jnp.float32)
        part = part * lmask[:, k : k + 1]
        total = total + jnp.sum((part * part).reshape(15, 8, TILE), axis=0)
        whole = jnp.concatenate([part, jnp.zeros((8, TILE), jnp.float32)], axis=0)
        lg[x, pl.ds(myrow, ROWS_P), k * TILE : k * TILE + TILE] = whole.astype(jnp.bfloat16)
    occx[x] = total

    def half(panel, low):
        return lg.at[panel, pl.ds(pl.multiple_of(myrow + low, 64), 64), :]

    def lowrow(d, k):
        ahead = 0 if d > 0 else 64
        return 64 - ahead if k == 1 else ahead

    def lindex(d, k):
        return (0 if d > 0 else 3) + k

    def lsent(d, k):
        panel = (x - d + X) % X if k == 2 else x
        ref = half(panel, lowrow(d, k))
        return pltpu.make_async_remote_copy(
            src_ref=ref, dst_ref=ref, send_sem=lsend.at[lindex(d, k)],
            recv_sem=lrecv.at[lindex(d, k)], device_id=xdev(d % X), device_id_type=MESH,
        )

    def lpart(d, k):
        panel = (x - (2 * d if k == 2 else d) + X) % X
        return half(panel, lowrow(d, k))

    def lgot(d, k):
        here = lpart(d, k)
        return pltpu.make_async_copy(here, here, lrecv.at[lindex(d, k)])

    def lshare(d, k):
        ref = lpart(d, k)
        return pltpu.make_async_remote_copy(
            src_ref=ref, dst_ref=ref, send_sem=lsibs.at[lindex(d, k)],
            recv_sem=lsibr.at[lindex(d, k)], device_id=sib, device_id_type=MESH,
        )

    otherrow = pl.multiple_of((1 - c) * ROWS_P, ROWS_P)

    def lshared(d, k):
        panel = (x - (2 * d if k == 2 else d) + X) % X
        here = lg.at[panel, pl.ds(pl.multiple_of(otherrow + lowrow(d, k), 64), 64), :]
        return pltpu.make_async_copy(here, here, lsibr.at[lindex(d, k)])

    mine = lg.at[x, pl.ds(myrow, ROWS_P), :]
    share_own = pltpu.make_async_remote_copy(
        src_ref=mine, dst_ref=mine, send_sem=lsibs.at[6], recv_sem=lsibr.at[6],
        device_id=sib, device_id_type=MESH,
    )

    for k in range(2):
        for d in ways:
            lsent(d, k).start()
    share_own.start()

    swapped(0).wait()
    for d in ways:
        sent(d, 0, 1).start()
    swapped(1).wait()
    for k in range(EARLY):
        for d in ways:
            sent(d, 1, k).start()

    def osent(stage, i, buf, slot, device):
        return pltpu.make_async_remote_copy(
            src_ref=buf.at[slot], dst_ref=buf.at[slot], send_sem=osend.at[i],
            recv_sem=orecv.at[stage], device_id=device, device_id_type=MESH,
        )

    stage_sends = [
        [osent(0, d - 1, occx, x, xdev(d)) for d in range(1, X)],
        [osent(1, 2 + d, occy, y, ydev(d)) for d in range(1, Y)],
        [osent(2, 10, occc, c, sib)],
        [osent(3, 10 + d, occz, z, (r, x, (z + d) % Z)) for d in range(1, Z)],
    ]

    def ogot(stage, buf, n):
        here = buf.at[pl.ds(0, n)]
        pltpu.make_async_copy(here, here, orecv.at[stage]).wait()

    for copy in stage_sends[0]:
        copy.start()

    tabk = one_hot(keep_ref[...] > 0)
    cols_in = one_hot(
        lax.broadcasted_iota(jnp.int32, (15, TILE), 0)
        == (lax.broadcasted_iota(jnp.int32, (15, TILE), 1) + x * COLS + z * OUT) // TILE
    )
    keepm[...] = dot(rows_in, dot(tabk, cols_in).astype(jnp.bfloat16))
    flag = jnp.where(branch_ref[...] > 0, 1.0, 0.0)
    branchm[...] = jnp.broadcast_to(
        jnp.sum(rows_in.astype(jnp.float32) * flag, axis=1, keepdims=True), (ROWS, TILE)
    )

    def multiply(t, step, begin=False):
        yy = (y + step + Y) % Y
        window = pl.multiple_of((yy % 2) * 1024, 1024)
        product = dot(lg[yy // 2, :, pl.ds(window, KWIN)], rb[t, yy])
        if begin:
            acc[t] = product
        else:
            acc[t] += product

    def scatter(t, run):
        for n in range(2):

            @pl.when(c == n)
            def _():
                i = t * 8
                for zd, low, rows, at in segments(2 * n + t):
                    for cd in range(2):
                        src = ct.at[t, cd, pl.ds(low, rows), :]
                        dst = zin.at[z, pl.ds(at, rows), :]
                        far = pltpu.make_async_remote_copy(
                            src_ref=src, dst_ref=dst, send_sem=zsend.at[i], recv_sem=zrecv.at[0],
                            device_id=(y * 2 + cd, x, jnp.int32(zd)), device_id_type=MESH,
                        )
                        if cd == n:

                            @pl.when(z != zd)
                            def _():
                                far.start() if run else far.wait_send()

                            if run:

                                @pl.when(z == zd)
                                def _():
                                    pltpu.make_async_copy(src, dst, zrecv.at[0]).start()
                        else:
                            far.start() if run else far.wait_send()
                        i += 1

    def turn(t):
        for cd in range(2):
            ct[t, cd] = acc[t, cd * TILE : cd * TILE + TILE, :].T

    for t in range(2):
        for k in range(7):
            for d in ways:
                got(d, t, k).wait()
                if k < 4:
                    sent(d, t, k + 2).start()
                if k == (4 if d > 0 else 5):
                    sent(d, t, 6).start()
                if t == 0 and k == 4:
                    for j in range(EARLY, 2):
                        sent(d, 1, j).start()
            if (t, k) == (0, 1):
                for d in ways:
                    lgot(d, 0).wait()
                    lsent(d, 2).start()
                    lshare(d, 0).start()
            if (t, k) == (0, 2):
                ogot(0, occx, X - 1)
                occy[y] = occx[0] + occx[1] + occx[2] + occx[3]
                for copy in stage_sends[1]:
                    copy.start()
            if (t, k) == (0, 4):
                for d in ways:
                    lgot(d, 1).wait()
                    lshare(d, 1).start()
            if (t, k) == (0, 5):
                ogot(1, occy, Y - 1)
                plane = occy[0]
                for j in range(1, Y):
                    plane = plane + occy[j]
                occc[c] = plane
                stage_sends[2][0].start()
            if (t, k) == (0, 6):
                for d in ways:
                    lgot(d, 2).wait()
                    lshare(d, 2).start()
                ogot(2, occc, 1)
                occz[z] = occc[0] + occc[1]
                for copy in stage_sends[3]:
                    copy.start()
            if (t, k) == (1, 0):
                for d in ways:
                    for j in range(3):
                        lshared(d, j).wait()
                pltpu.make_async_copy(mine, mine, lsibr.at[6]).wait()
                for j in range(2):
                    keep_own(j).wait()
                multiply(0, 0, True)
                multiply(0, 1)
                multiply(0, -1)
            if (t, k) == (1, 1):
                multiply(0, 2)
                multiply(0, -2)
                multiply(0, 3)
            if (t, k) == (1, 2):
                multiply(0, -3)
                multiply(0, 4)
                turn(0)
                scatter(0, True)
            if (t, k) == (1, 3):
                multiply(1, 0, True)
                multiply(1, 1)
                multiply(1, -1)
            if (t, k) == (1, 4):
                multiply(1, 2)
                multiply(1, -2)
            if (t, k) == (1, 5):
                multiply(1, 3)
                multiply(1, -3)
            if (t, k) == (1, 6):
                multiply(1, 4)
                turn(1)
                scatter(1, True)

    ogot(3, occz, Z - 1)
    whole = occz[0]
    for j in range(1, Z):
        whole = whole + occz[j]
    mean = jnp.sum(whole, keepdims=True) / float(ROWS * 2 * Y)
    occ_ref[...] = jnp.broadcast_to(mean, (8, TILE))

    for d in ways:
        for t in range(2):
            for k in range(7):
                sent(d, t, k).wait_send()
        for k in range(3):
            lsent(d, k).wait_send()
            lshare(d, k).wait_send()
    for t in range(2):
        swap(t).wait_send()
    share_own.wait_send()
    for copies in stage_sends:
        for copy in copies:
            copy.wait_send()

    pltpu.make_async_copy(zin, zin, zrecv.at[0]).wait()
    square = zin[0]
    for j in range(1, Z):
        square = square + zin[j]
    square = jnp.concatenate([square, jnp.zeros((TILE - OUT, TILE), jnp.float32)], axis=0).T
    square = square[:ROWS, :OUT]
    doubled = 2.0 * win_ref[...].astype(jnp.float32) - square
    updated = jnp.where(branchm[:, :OUT] > 0.5, doubled, square)
    out_ref[...] = jnp.where(keepm[:, :OUT] > 0.5, updated, 0.0).astype(jnp.bfloat16)
    for t in range(2):
        scatter(t, False)


def shards(row_stripe, column_stripe, window_block, stripe_tiles, column_tiles, keep_tiles, branch):
    bf, f32 = jnp.bfloat16, jnp.float32
    dma = pltpu.SemaphoreType.DMA
    vmem = pl.BlockSpec(memory_space=pltpu.VMEM)
    block, occupancy = pl.pallas_call(
        kernel,
        out_shape=(
            jax.ShapeDtypeStruct((ROWS, OUT), bf),
            jax.ShapeDtypeStruct((8, TILE), f32),
        ),
        in_specs=[vmem] * 7,
        out_specs=(vmem, vmem),
        scratch_shapes=[
            pltpu.VMEM((4, SUB, TILE), bf),
            pltpu.VMEM((2, Y, KWIN, TILE), bf),
            pltpu.VMEM((X, 2 * ROWS_P, PANEL), bf),
            pltpu.VMEM((2, 2 * ROWS_P, TILE), f32),
            pltpu.VMEM((2, 2, TILE, TILE), f32),
            pltpu.VMEM((Z, OUT, TILE), f32),
            pltpu.VMEM((X, 8, TILE), f32),
            pltpu.VMEM((Y, 8, TILE), f32),
            pltpu.VMEM((2, 8, TILE), f32),
            pltpu.VMEM((Z, 8, TILE), f32),
            pltpu.VMEM((ROWS, TILE), f32),
            pltpu.VMEM((ROWS, TILE), f32),
            dma((28,)), dma((28,)),
            dma((2,)), dma((2,)), dma((2,)),
            dma((6,)), dma((6,)), dma((7,)), dma((7,)),
            dma((16,)), dma((1,)),
            dma((22,)), dma((4,)),
        ],
        compiler_params=pltpu.CompilerParams(
            collective_id=0, has_side_effects=True, vmem_limit_bytes=32 * 2**20
        ),
        name="square",
    )(row_stripe, column_stripe, window_block, stripe_tiles, column_tiles, keep_tiles, branch[None, :])
    return block, occupancy[0, 0]


def solution(mesh):
    return jax.shard_map(
        shards,
        mesh=mesh,
        in_specs=(
            P("row", "depth", "col"),
            P("depth", "row", "col"),
            P("row", ("col", "depth")),
            P(),
            P(),
            P(),
            P(),
        ),
        out_specs=(P("row", ("col", "depth")), P()),
        check_vma=False,
    )
```

```python
import functools

import jax
import jax.numpy as jnp
from jax import lax
from jax.experimental import pallas as pl
from jax.experimental.pallas import tpu as pltpu
from jax.sharding import PartitionSpec as P

TILE = 128
MESH = pl.DeviceIdType.MESH
X, Y, Z = 4, 8, 12
ROWS = 120
ROWS_P = 128
PANEL = 2176
SUB = 544
COLS = 480
OUT = 40
KWIN = 1152
PART = 272
EARLY = 4
STEPS = 14


def segments(tile):
    found = []
    for z in range(Z):
        low = max(tile * TILE, z * OUT)
        high = min(tile * TILE + TILE, COLS, z * OUT + OUT)
        if low < high:
            found.append((z, low - tile * TILE, high - low, low - z * OUT))
    return found


def one_hot(hit):
    return jnp.where(hit, 1.0, 0.0).astype(jnp.bfloat16)


def dot(a, b):
    return jnp.dot(a, b, preferred_element_type=jnp.float32)


def dot_t(a, b):
    dims = (((1,), (1,)), ((), ()))
    return lax.dot_general(a, b, dims, preferred_element_type=jnp.float32)


def kernel(
    row_in, col_in, win_in, stripe_in, ctab_in, keep_in, branch_in,
    out_ref, occ_ref,
    row_ref, col_ref, win_ref, stripe_ref, ctab_ref, keep_ref, branch_ref, in_sem,
    rm, rb, lg, acc, ct, zin, occx, occy, occc, occz, keepm, branchm,
    rsend, rrecv, go, dsend, drecv, own_sem, lsend, lrecv, lsibs, lsibr, zsend, zrecv, osend, orecv,
):
    r = lax.axis_index("row")
    x = lax.axis_index("col")
    z = lax.axis_index("depth")
    y = r // 2
    c = r % 2

    def ydev(d):
        return (((y + d) % Y) * 2 + c, x, z)

    def xdev(d):
        return (r, (x + d) % X, z)

    sib = (y * 2 + (1 - c), x, z)

    arrays = [
        (ctab_in, ctab_ref), (col_in, col_ref), (stripe_in, stripe_ref), (row_in, row_ref),
        (keep_in, keep_ref), (branch_in, branch_ref), (win_in, win_ref),
    ]
    loads = [pltpu.make_async_copy(a, b, in_sem.at[i]) for i, (a, b) in enumerate(arrays)]
    for load in loads:
        load.start()

    barrier = pltpu.get_barrier_semaphore()
    plane = [((y + d) % Y * 2, x, z) for d in range(1, Y)] + [(y * 2, (x + d) % X, z) for d in range(1, X)]
    others = [(y * 2 + 1, x, (z + d) % Z) for d in range(1, Z)]
    for peer in plane:
        pl.semaphore_signal(barrier, inc=1, device_id=peer, device_id_type=MESH)

    @pl.when(c == 1)
    def _():
        pl.semaphore_signal(barrier, inc=1, device_id=sib, device_id_type=MESH)

    for peer in others:
        pl.semaphore_signal(barrier, inc=1, device_id=peer, device_id_type=MESH)

    def agree(counter, count, i):
        @pl.when(c == counter)
        def _():
            pl.semaphore_wait(barrier, count)
            pl.semaphore_signal(go.at[i], inc=1, device_id=sib, device_id_type=MESH)

        @pl.when(c != counter)
        def _():
            pl.semaphore_wait(go.at[i], 1)

    for t in range(2):
        for yy in range(Y):
            low = 0 if yy % 2 else 2 * SUB
            rb[t, yy, low : low + 64, :] = jnp.zeros((64, TILE), jnp.bfloat16)

    first = z * 68 + (r * SUB) // TILE
    skew = (r * SUB) % TILE
    loads[0].wait()
    ctab = one_hot(ctab_ref[...] > 0)
    pick = one_hot(
        lax.broadcasted_iota(jnp.int32, (16, 816), 1)
        == lax.broadcasted_iota(jnp.int32, (16, 816), 0) + first
    )
    picked = dot_t(pick, ctab).astype(jnp.bfloat16)
    spread = one_hot(
        lax.broadcasted_iota(jnp.int32, (15, 512), 0)
        == (lax.broadcasted_iota(jnp.int32, (15, 512), 1) + x * COLS) // TILE
    )
    by_col = dot(picked, spread).astype(jnp.bfloat16)
    band = one_hot(
        lax.broadcasted_iota(jnp.int32, (SUB, 16), 1)
        == (lax.broadcasted_iota(jnp.int32, (SUB, 16), 0) + skew) // TILE
    )

    def masked(tile):
        wide = min(TILE, COLS - tile * TILE)
        if wide < TILE:
            rm[tile] = jnp.zeros((SUB, TILE), jnp.bfloat16)
        mask = dot(band, by_col[:, tile * TILE : tile * TILE + wide]).astype(jnp.bfloat16)
        rm[tile, :, 0:wide] = col_ref[:, tile * TILE : tile * TILE + wide] * mask

    loads[1].wait()
    masked(0)
    masked(1)

    agree(0, 2 * len(plane) + 1, 0)

    def off(yy, cc):
        return pl.multiple_of((yy % 2) * 64 + cc * SUB, 32)

    def piece(t, yy, cc, part=None):
        if part is None:
            return rb.at[t, yy, pl.ds(off(yy, cc), SUB), :]
        return rb.at[t, yy, pl.ds(pl.multiple_of(off(yy, cc) + part * PART, 16), PART), :]

    def which(d, k):
        if k >= 12:
            return (c if d > 0 else 1 - c), k % 2
        return (c if k % 4 < 2 else 1 - c), k % 2

    def sent(d, t, k):
        yy = (y - d * (k // 4) + Y) % Y
        core, part = which(d, k)
        there = piece(t, yy, core, part)
        here = rm.at[2 * t + c, part * PART : (part + 1) * PART, :] if k < 2 else there
        i = ((0 if d > 0 else 2) + t) * STEPS + k
        return pltpu.make_async_remote_copy(
            src_ref=here, dst_ref=there, send_sem=rsend.at[i], recv_sem=rrecv.at[i],
            device_id=ydev(d % Y), device_id_type=MESH,
        )

    def got(d, t, k):
        yy = (y - d * (k // 4 + 1) + Y) % Y
        here = piece(t, yy, *which(d, k))
        i = ((0 if d > 0 else 2) + t) * STEPS + k
        return pltpu.make_async_copy(here, here, rrecv.at[i])

    ways = (1, -1)
    for k in range(2):
        for d in ways:
            sent(d, 0, k).start()

    def swap(t):
        return pltpu.make_async_remote_copy(
            src_ref=rm.at[2 * t + 1 - c], dst_ref=piece(t, y, c),
            send_sem=dsend.at[t], recv_sem=drecv.at[t], device_id=sib, device_id_type=MESH,
        )

    def keep_own(t):
        return pltpu.make_async_copy(rm.at[2 * t + c], piece(t, y, c), own_sem.at[t])

    def swapped(t):
        here = piece(t, y, 1 - c)
        return pltpu.make_async_copy(here, here, drecv.at[t])

    swap(0).start()
    keep_own(0).start()
    masked(2)
    masked(3)
    swap(1).start()
    keep_own(1).start()

    loads[2].wait()
    loads[3].wait()
    stab = one_hot(stripe_ref[...] > 0)
    base = z * 68 + x * 17
    shift = one_hot(
        lax.broadcasted_iota(jnp.int32, (816, TILE), 0)
        == lax.broadcasted_iota(jnp.int32, (816, TILE), 1) + base
    )
    narrow = dot(stab, shift).astype(jnp.bfloat16)
    rows_in = one_hot(
        lax.broadcasted_iota(jnp.int32, (ROWS, 15), 1)
        == (lax.broadcasted_iota(jnp.int32, (ROWS, 15), 0) + r * ROWS) // TILE
    )
    lmask = dot(rows_in, narrow)
    total = jnp.zeros((8, TILE), jnp.float32)
    myrow = pl.multiple_of(c * ROWS_P, ROWS_P)
    for k in range(17):
        part = row_ref[:, k * TILE : k * TILE + TILE].astype(jnp.float32)
        part = part * lmask[:, k : k + 1]
        total = total + jnp.sum((part * part).reshape(15, 8, TILE), axis=0)
        whole = jnp.concatenate([part, jnp.zeros((8, TILE), jnp.float32)], axis=0)
        lg[x, pl.ds(myrow, ROWS_P), k * TILE : k * TILE + TILE] = whole.astype(jnp.bfloat16)
    occx[x] = total

    def half(panel, low):
        return lg.at[panel, pl.ds(pl.multiple_of(myrow + low, 64), 64), :]

    def lowrow(d, k):
        ahead = 0 if d > 0 else 64
        return 64 - ahead if k == 1 else ahead

    def lindex(d, k):
        return (0 if d > 0 else 3) + k

    def lsent(d, k):
        panel = (x - d + X) % X if k == 2 else x
        ref = half(panel, lowrow(d, k))
        return pltpu.make_async_remote_copy(
            src_ref=ref, dst_ref=ref, send_sem=lsend.at[lindex(d, k)],
            recv_sem=lrecv.at[lindex(d, k)], device_id=xdev(d % X), device_id_type=MESH,
        )

    def lpart(d, k):
        panel = (x - (2 * d if k == 2 else d) + X) % X
        return half(panel, lowrow(d, k))

    def lgot(d, k):
        here = lpart(d, k)
        return pltpu.make_async_copy(here, here, lrecv.at[lindex(d, k)])

    def lshare(d, k):
        ref = lpart(d, k)
        return pltpu.make_async_remote_copy(
            src_ref=ref, dst_ref=ref, send_sem=lsibs.at[lindex(d, k)],
            recv_sem=lsibr.at[lindex(d, k)], device_id=sib, device_id_type=MESH,
        )

    otherrow = pl.multiple_of((1 - c) * ROWS_P, ROWS_P)

    def lshared(d, k):
        panel = (x - (2 * d if k == 2 else d) + X) % X
        here = lg.at[panel, pl.ds(pl.multiple_of(otherrow + lowrow(d, k), 64), 64), :]
        return pltpu.make_async_copy(here, here, lsibr.at[lindex(d, k)])

    mine = lg.at[x, pl.ds(myrow, ROWS_P), :]
    share_own = pltpu.make_async_remote_copy(
        src_ref=mine, dst_ref=mine, send_sem=lsibs.at[6], recv_sem=lsibr.at[6],
        device_id=sib, device_id_type=MESH,
    )

    for k in range(2):
        for d in ways:
            lsent(d, k).start()
    share_own.start()

    swapped(0).wait()
    for k in range(2, 4):
        for d in ways:
            sent(d, 0, k).start()
    swapped(1).wait()
    for k in range(EARLY):
        for d in ways:
            sent(d, 1, k).start()

    def osent(stage, i, buf, slot, device):
        return pltpu.make_async_remote_copy(
            src_ref=buf.at[slot], dst_ref=buf.at[slot], send_sem=osend.at[i],
            recv_sem=orecv.at[stage], device_id=device, device_id_type=MESH,
        )

    stage_sends = [
        [osent(0, d - 1, occx, x, xdev(d)) for d in range(1, X)],
        [osent(1, 2 + d, occy, y, ydev(d)) for d in range(1, Y)],
        [osent(2, 10, occc, c, sib)],
        [osent(3, 10 + d, occz, z, (r, x, (z + d) % Z)) for d in range(1, Z)],
    ]

    def ogot(stage, buf, n):
        here = buf.at[pl.ds(0, n)]
        pltpu.make_async_copy(here, here, orecv.at[stage]).wait()

    for copy in stage_sends[0]:
        copy.start()

    for load in loads[4:]:
        load.wait()
    tabk = one_hot(keep_ref[...] > 0)
    cols_in = one_hot(
        lax.broadcasted_iota(jnp.int32, (OUT, 15), 1)
        == (lax.broadcasted_iota(jnp.int32, (OUT, 15), 0) + x * COLS + z * OUT) // TILE
    )
    across = one_hot(
        lax.broadcasted_iota(jnp.int32, (15, ROWS), 0)
        == (lax.broadcasted_iota(jnp.int32, (15, ROWS), 1) + r * ROWS) // TILE
    )
    keepm[...] = dot(dot_t(cols_in, tabk).astype(jnp.bfloat16), across)
    flag = jnp.broadcast_to(one_hot(branch_ref[...] > 0), (OUT, 15))
    branchm[...] = dot(flag, across)

    def multiply(t, step, begin=False):
        yy = (y + step + Y) % Y
        window = pl.multiple_of((yy % 2) * 1024, 1024)
        product = dot(lg[yy // 2, :, pl.ds(window, KWIN)], rb[t, yy])
        if begin:
            acc[t] = product
        else:
            acc[t] += product

    def scatter(t, run):
        for n in range(2):

            @pl.when(c == n)
            def _():
                i = t * 8
                for zd, low, rows, at in segments(2 * t + n):
                    for cd in range(2):
                        src = ct.at[t, cd, pl.ds(low, rows), :]
                        dst = zin.at[z, pl.ds(at, rows), :]
                        far = pltpu.make_async_remote_copy(
                            src_ref=src, dst_ref=dst, send_sem=zsend.at[i], recv_sem=zrecv.at[0],
                            device_id=(y * 2 + cd, x, jnp.int32(zd)), device_id_type=MESH,
                        )
                        if cd == n:

                            @pl.when(z != zd)
                            def _():
                                far.start() if run else far.wait_send()

                            if run:

                                @pl.when(z == zd)
                                def _():
                                    pltpu.make_async_copy(src, dst, zrecv.at[0]).start()
                        else:
                            far.start() if run else far.wait_send()
                        i += 1

    def turn(t):
        for cd in range(2):
            ct[t, cd] = acc[t, cd * TILE : cd * TILE + TILE, :].T

    for t in range(2):
        for k in range(STEPS):
            for d in ways:
                got(d, t, k).wait()
                if k < 8:
                    sent(d, t, k + 4).start()
                if k in ((8, 9) if d > 0 else (10, 11)):
                    sent(d, t, 12 + k % 2).start()
                if t == 0 and k == 8:
                    for j in range(EARLY, 4):
                        sent(d, 1, j).start()
            if (t, k) == (0, 2):
                for d in ways:
                    lgot(d, 0).wait()
                    lsent(d, 2).start()
                    lshare(d, 0).start()
            if (t, k) == (0, 4):
                ogot(0, occx, X - 1)
                occy[y] = occx[0] + occx[1] + occx[2] + occx[3]
                for copy in stage_sends[1]:
                    copy.start()
            if (t, k) == (0, 6):
                for d in ways:
                    lgot(d, 1).wait()
                    lshare(d, 1).start()
            if (t, k) == (0, 8):
                ogot(1, occy, Y - 1)
                summed = occy[0]
                for j in range(1, Y):
                    summed = summed + occy[j]
                occc[c] = summed
                stage_sends[2][0].start()
            if (t, k) == (0, 10):
                for d in ways:
                    lgot(d, 2).wait()
                    lshare(d, 2).start()
            if (t, k) == (0, 11):
                ogot(2, occc, 1)
                occz[z] = occc[0] + occc[1]
                agree(1, 2 * len(others), 1)
                for copy in stage_sends[3]:
                    copy.start()
            if (t, k) == (0, 12):
                for d in ways:
                    for j in range(3):
                        lshared(d, j).wait()
                pltpu.make_async_copy(mine, mine, lsibr.at[6]).wait()
                for j in range(2):
                    keep_own(j).wait()
                multiply(0, 0, True)
                multiply(0, 1)
                multiply(0, -1)
            if (t, k) == (0, 13):
                multiply(0, 2)
                multiply(0, -2)
            if (t, k) == (1, 1):
                multiply(0, 3)
                multiply(0, -3)
            if (t, k) == (1, 3):
                multiply(0, 4)
                turn(0)
                scatter(0, True)
            if (t, k) == (1, 5):
                multiply(1, 0, True)
            if (t, k) == (1, 6):
                multiply(1, 1)
            if (t, k) == (1, 7):
                multiply(1, -1)
            if (t, k) == (1, 8):
                multiply(1, 2)
            if (t, k) == (1, 9):
                multiply(1, -2)
            if (t, k) == (1, 11):
                multiply(1, 3)
                multiply(1, -3)
            if (t, k) == (1, 13):
                multiply(1, 4)
                turn(1)
                scatter(1, True)

    ogot(3, occz, Z - 1)
    whole = occz[0]
    for j in range(1, Z):
        whole = whole + occz[j]
    mean = jnp.sum(whole, keepdims=True) / float(ROWS * 2 * Y)
    occ_ref[...] = mean

    for d in ways:
        for t in range(2):
            for k in range(STEPS):
                sent(d, t, k).wait_send()
        for k in range(3):
            lsent(d, k).wait_send()
            lshare(d, k).wait_send()
    for t in range(2):
        swap(t).wait_send()
    share_own.wait_send()
    for copies in stage_sends:
        for copy in copies:
            copy.wait_send()

    pltpu.make_async_copy(zin, zin, zrecv.at[0]).wait()
    square = zin[0]
    for j in range(1, Z):
        square = square + zin[j]
    square = square[:, :ROWS]
    doubled = 2.0 * win_ref[...].astype(jnp.float32) - square
    updated = jnp.where(branchm[...] > 0.5, doubled, square)
    out_ref[...] = jnp.where(keepm[...] > 0.5, updated, 0.0).astype(jnp.bfloat16)
    for t in range(2):
        scatter(t, False)


def shards(row_stripe, column_stripe, window_block, stripe_tiles, column_tiles, keep_tiles, branch):
    bf, f32 = jnp.bfloat16, jnp.float32
    dma = pltpu.SemaphoreType.DMA
    vmem = pl.BlockSpec(memory_space=pltpu.VMEM)
    block, occupancy = pl.pallas_call(
        kernel,
        out_shape=(
            jax.ShapeDtypeStruct((OUT, ROWS), bf),
            jax.ShapeDtypeStruct((1, 1), f32),
        ),
        in_specs=[pl.BlockSpec(memory_space=pl.ANY)] * 7,
        out_specs=(vmem, vmem),
        scratch_shapes=[
            pltpu.VMEM((ROWS, PANEL), bf),
            pltpu.VMEM((SUB, COLS), bf),
            pltpu.VMEM((OUT, ROWS), bf),
            pltpu.VMEM((15, 816), jnp.int32),
            pltpu.VMEM((15, 816), jnp.int32),
            pltpu.VMEM((15, 15), jnp.int32),
            pltpu.VMEM((1, 15), jnp.int32),
            dma((7,)),
            pltpu.VMEM((4, SUB, TILE), bf),
            pltpu.VMEM((2, Y, KWIN, TILE), bf),
            pltpu.VMEM((X, 2 * ROWS_P, PANEL), bf),
            pltpu.VMEM((2, 2 * ROWS_P, TILE), f32),
            pltpu.VMEM((2, 2, TILE, TILE), f32),
            pltpu.VMEM((Z, OUT, TILE), f32),
            pltpu.VMEM((X, 8, TILE), f32),
            pltpu.VMEM((Y, 8, TILE), f32),
            pltpu.VMEM((2, 8, TILE), f32),
            pltpu.VMEM((Z, 8, TILE), f32),
            pltpu.VMEM((OUT, ROWS), f32),
            pltpu.VMEM((OUT, ROWS), f32),
            dma((4 * STEPS,)), dma((4 * STEPS,)), pltpu.SemaphoreType.REGULAR((2,)),
            dma((2,)), dma((2,)), dma((2,)),
            dma((6,)), dma((6,)), dma((7,)), dma((7,)),
            dma((16,)), dma((1,)),
            dma((22,)), dma((4,)),
        ],
        compiler_params=pltpu.CompilerParams(
            collective_id=0, has_side_effects=True, vmem_limit_bytes=56 * 2**20
        ),
        name="square",
    )(
        row_stripe[:, 0, :], column_stripe[0], window_block.T, stripe_tiles, column_tiles.T,
        keep_tiles, branch[None, :],
    )
    return block.T, occupancy[0, 0]


def solution(mesh):
    return jax.shard_map(
        shards,
        mesh=mesh,
        in_specs=(
            P("row", "depth", "col"),
            P("depth", "row", "col"),
            P("row", ("col", "depth")),
            P(),
            P(),
            P(),
            P(),
        ),
        out_specs=(P("row", ("col", "depth")), P()),
        check_vma=False,
    )
```

```python
import functools

import jax
import jax.numpy as jnp
from jax import lax
from jax.experimental import pallas as pl
from jax.experimental.pallas import tpu as pltpu
from jax.sharding import PartitionSpec as P

TILE = 128
MESH = pl.DeviceIdType.MESH
X, Y, Z = 4, 8, 12
ROWS = 120
ROWS_P = 128
PANEL = 2176
SUB = 544
COLS = 480
OUT = 40
KWIN = 1152
PART = 272
EARLY = 3
STEPS = 14


def segments(tile):
    found = []
    for z in range(Z):
        low = max(tile * TILE, z * OUT)
        high = min(tile * TILE + TILE, COLS, z * OUT + OUT)
        if low < high:
            found.append((z, low - tile * TILE, high - low, low - z * OUT))
    return found


def one_hot(hit):
    return jnp.where(hit, 1.0, 0.0).astype(jnp.bfloat16)


def dot(a, b):
    return jnp.dot(a, b, preferred_element_type=jnp.float32)


def dot_t(a, b):
    dims = (((1,), (1,)), ((), ()))
    return lax.dot_general(a, b, dims, preferred_element_type=jnp.float32)


def kernel(
    row_in, col_in, win_in, stripe_in, ctab_in, keep_in, branch_in,
    out_ref, occ_ref,
    row_ref, col_ref, win_ref, stripe_ref, ctab_ref, keep_ref, branch_ref, in_sem,
    rm, rb, lg, acc, ct, zin, occx, occy, occc, occz, keepm, branchm,
    rsend, rrecv, go, dsend, drecv, own_sem, lsend, lrecv, lsibs, lsibr, zsend, zrecv, osend, orecv,
):
    r = lax.axis_index("row")
    x = lax.axis_index("col")
    z = lax.axis_index("depth")
    y = r // 2
    c = r % 2

    def ydev(d):
        return (((y + d) % Y) * 2 + c, x, z)

    def xdev(d):
        return (r, (x + d) % X, z)

    sib = (y * 2 + (1 - c), x, z)

    arrays = [
        (ctab_in, ctab_ref), (col_in, col_ref), (stripe_in, stripe_ref), (row_in, row_ref),
        (keep_in, keep_ref), (branch_in, branch_ref), (win_in, win_ref),
    ]
    loads = [pltpu.make_async_copy(a, b, in_sem.at[i]) for i, (a, b) in enumerate(arrays)]
    for load in loads:
        load.start()

    barrier = pltpu.get_barrier_semaphore()
    plane = [((y + d) % Y * 2, x, z) for d in range(1, Y)] + [(y * 2, (x + d) % X, z) for d in range(1, X)]
    others = [(y * 2 + 1, x, (z + d) % Z) for d in range(1, Z)]
    for peer in plane:
        pl.semaphore_signal(barrier, inc=1, device_id=peer, device_id_type=MESH)

    @pl.when(c == 1)
    def _():
        pl.semaphore_signal(barrier, inc=1, device_id=sib, device_id_type=MESH)

    def agree(counter, count, i):
        @pl.when(c == counter)
        def _():
            pl.semaphore_wait(barrier, count)
            pl.semaphore_signal(go.at[i], inc=1, device_id=sib, device_id_type=MESH)

        @pl.when(c != counter)
        def _():
            pl.semaphore_wait(go.at[i], 1)

    for t in range(2):
        for yy in range(Y):
            low = 0 if yy % 2 else 2 * SUB
            rb[t, yy, low : low + 64, :] = jnp.zeros((64, TILE), jnp.bfloat16)

    first = z * 68 + (r * SUB) // TILE
    skew = (r * SUB) % TILE
    loads[0].wait()
    ctab = one_hot(ctab_ref[...] > 0)
    pick = one_hot(
        lax.broadcasted_iota(jnp.int32, (16, 816), 1)
        == lax.broadcasted_iota(jnp.int32, (16, 816), 0) + first
    )
    picked = dot_t(pick, ctab).astype(jnp.bfloat16)
    spread = one_hot(
        lax.broadcasted_iota(jnp.int32, (15, 512), 0)
        == (lax.broadcasted_iota(jnp.int32, (15, 512), 1) + x * COLS) // TILE
    )
    by_col = dot(picked, spread).astype(jnp.bfloat16)
    band = one_hot(
        lax.broadcasted_iota(jnp.int32, (SUB, 16), 1)
        == (lax.broadcasted_iota(jnp.int32, (SUB, 16), 0) + skew) // TILE
    )

    def masked(tile):
        wide = min(TILE, COLS - tile * TILE)
        if wide < TILE:
            rm[tile] = jnp.zeros((SUB, TILE), jnp.bfloat16)
        mask = dot(band, by_col[:, tile * TILE : tile * TILE + wide]).astype(jnp.bfloat16)
        rm[tile, :, 0:wide] = col_ref[:, tile * TILE : tile * TILE + wide] * mask

    loads[1].wait()
    for n in range(2):

        @pl.when(c == n)
        def _():
            masked(n)

    agree(0, 2 * len(plane) + 1, 0)

    def off(yy, cc):
        return pl.multiple_of((yy % 2) * 64 + cc * SUB, 32)

    def piece(t, yy, cc, part=None):
        if part is None:
            return rb.at[t, yy, pl.ds(off(yy, cc), SUB), :]
        return rb.at[t, yy, pl.ds(pl.multiple_of(off(yy, cc) + part * PART, 16), PART), :]

    def which(d, k):
        if k >= 8 and d < 0:
            return (1 - c if k % 4 < 2 else c), k % 2
        return (c if k % 4 < 2 else 1 - c), k % 2

    def sent(d, t, k):
        yy = (y - d * (k // 4) + Y) % Y
        core, part = which(d, k)
        there = piece(t, yy, core, part)
        here = rm.at[2 * t + c, part * PART : (part + 1) * PART, :] if k < 2 else there
        i = ((0 if d > 0 else 2) + t) * STEPS + k
        return pltpu.make_async_remote_copy(
            src_ref=here, dst_ref=there, send_sem=rsend.at[i], recv_sem=rrecv.at[i],
            device_id=ydev(d % Y), device_id_type=MESH,
        )

    def passed(d, k):
        if 4 <= k < 8 and d < 0:
            return 8 + (k - 4 + 2) % 4
        return k + 4

    def got(d, t, k):
        yy = (y - d * (k // 4 + 1) + Y) % Y
        here = piece(t, yy, *which(d, k))
        i = ((0 if d > 0 else 2) + t) * STEPS + k
        return pltpu.make_async_copy(here, here, rrecv.at[i])

    ways = (1, -1)
    for k in range(2):
        for d in ways:
            sent(d, 0, k).start()

    def swap(t):
        return pltpu.make_async_remote_copy(
            src_ref=rm.at[2 * t + 1 - c], dst_ref=piece(t, y, c),
            send_sem=dsend.at[t], recv_sem=drecv.at[t], device_id=sib, device_id_type=MESH,
        )

    def keep_own(t):
        return pltpu.make_async_copy(rm.at[2 * t + c], piece(t, y, c), own_sem.at[t])

    def swapped(t):
        here = piece(t, y, 1 - c)
        return pltpu.make_async_copy(here, here, drecv.at[t])

    for n in range(2):

        @pl.when(c != n)
        def _():
            masked(n)

    swap(0).start()
    keep_own(0).start()
    for peer in others:
        pl.semaphore_signal(barrier, inc=1, device_id=peer, device_id_type=MESH)
    masked(2)
    masked(3)
    swap(1).start()
    keep_own(1).start()

    loads[2].wait()
    loads[3].wait()
    stab = one_hot(stripe_ref[...] > 0)
    base = z * 68 + x * 17
    shift = one_hot(
        lax.broadcasted_iota(jnp.int32, (816, TILE), 0)
        == lax.broadcasted_iota(jnp.int32, (816, TILE), 1) + base
    )
    narrow = dot(stab, shift).astype(jnp.bfloat16)
    rows_in = one_hot(
        lax.broadcasted_iota(jnp.int32, (ROWS, 15), 1)
        == (lax.broadcasted_iota(jnp.int32, (ROWS, 15), 0) + r * ROWS) // TILE
    )
    lmask = dot(rows_in, narrow)
    total = jnp.zeros((8, TILE), jnp.float32)
    myrow = pl.multiple_of(c * ROWS_P, ROWS_P)
    for k in range(17):
        part = row_ref[:, k * TILE : k * TILE + TILE].astype(jnp.float32)
        part = part * lmask[:, k : k + 1]
        total = total + jnp.sum((part * part).reshape(15, 8, TILE), axis=0)
        whole = jnp.concatenate([part, jnp.zeros((8, TILE), jnp.float32)], axis=0)
        lg[x, pl.ds(myrow, ROWS_P), k * TILE : k * TILE + TILE] = whole.astype(jnp.bfloat16)
    occx[x] = total

    def half(panel, low):
        return lg.at[panel, pl.ds(pl.multiple_of(myrow + low, 64), 64), :]

    def lowrow(d, k):
        ahead = 0 if d > 0 else 64
        return 64 - ahead if k == 1 else ahead

    def lindex(d, k):
        return (0 if d > 0 else 3) + k

    def lsent(d, k):
        panel = (x - d + X) % X if k == 2 else x
        ref = half(panel, lowrow(d, k))
        return pltpu.make_async_remote_copy(
            src_ref=ref, dst_ref=ref, send_sem=lsend.at[lindex(d, k)],
            recv_sem=lrecv.at[lindex(d, k)], device_id=xdev(d % X), device_id_type=MESH,
        )

    def lpart(d, k):
        panel = (x - (2 * d if k == 2 else d) + X) % X
        return half(panel, lowrow(d, k))

    def lgot(d, k):
        here = lpart(d, k)
        return pltpu.make_async_copy(here, here, lrecv.at[lindex(d, k)])

    def lshare(d, k):
        ref = lpart(d, k)
        return pltpu.make_async_remote_copy(
            src_ref=ref, dst_ref=ref, send_sem=lsibs.at[lindex(d, k)],
            recv_sem=lsibr.at[lindex(d, k)], device_id=sib, device_id_type=MESH,
        )

    otherrow = pl.multiple_of((1 - c) * ROWS_P, ROWS_P)

    def lshared(d, k):
        panel = (x - (2 * d if k == 2 else d) + X) % X
        here = lg.at[panel, pl.ds(pl.multiple_of(otherrow + lowrow(d, k), 64), 64), :]
        return pltpu.make_async_copy(here, here, lsibr.at[lindex(d, k)])

    mine = lg.at[x, pl.ds(myrow, ROWS_P), :]
    share_own = pltpu.make_async_remote_copy(
        src_ref=mine, dst_ref=mine, send_sem=lsibs.at[6], recv_sem=lsibr.at[6],
        device_id=sib, device_id_type=MESH,
    )

    for k in range(2):
        for d in ways:
            lsent(d, k).start()
    share_own.start()

    swapped(0).wait()
    for k in range(2, 4):
        for d in ways:
            sent(d, 0, k).start()
    swapped(1).wait()
    for k in range(EARLY):
        for d in ways:
            sent(d, 1, k).start()

    def osent(stage, i, buf, slot, device):
        return pltpu.make_async_remote_copy(
            src_ref=buf.at[slot], dst_ref=buf.at[slot], send_sem=osend.at[i],
            recv_sem=orecv.at[stage], device_id=device, device_id_type=MESH,
        )

    stage_sends = [
        [osent(0, d - 1, occx, x, xdev(d)) for d in range(1, X)],
        [osent(1, 2 + d, occy, y, ydev(d)) for d in range(1, Y)],
        [osent(2, 10, occc, c, sib)],
        [osent(3, 10 + d, occz, z, (r, x, (z + d) % Z)) for d in range(1, Z)],
    ]

    def ogot(stage, buf, n):
        here = buf.at[pl.ds(0, n)]
        pltpu.make_async_copy(here, here, orecv.at[stage]).wait()

    for copy in stage_sends[0]:
        copy.start()

    for load in loads[4:]:
        load.wait()
    tabk = one_hot(keep_ref[...] > 0)
    cols_in = one_hot(
        lax.broadcasted_iota(jnp.int32, (OUT, 15), 1)
        == (lax.broadcasted_iota(jnp.int32, (OUT, 15), 0) + x * COLS + z * OUT) // TILE
    )
    across = one_hot(
        lax.broadcasted_iota(jnp.int32, (15, ROWS), 0)
        == (lax.broadcasted_iota(jnp.int32, (15, ROWS), 1) + r * ROWS) // TILE
    )
    keepm[...] = dot(dot_t(cols_in, tabk).astype(jnp.bfloat16), across)
    flag = jnp.broadcast_to(one_hot(branch_ref[...] > 0), (OUT, 15))
    branchm[...] = dot(flag, across)

    def multiply(t, step, begin=False):
        yy = (y + step + Y) % Y
        window = pl.multiple_of((yy % 2) * 1024, 1024)
        product = dot(lg[yy // 2, :, pl.ds(window, KWIN)], rb[t, yy])
        if begin:
            acc[t] = product
        else:
            acc[t] += product

    def scatter(t, run):
        for n in range(2):

            @pl.when(c == n)
            def _():
                i = t * 8
                for zd, low, rows, at in segments(2 * t + n):
                    for cd in range(2):
                        src = ct.at[t, cd, pl.ds(low, rows), :]
                        dst = zin.at[z, pl.ds(at, rows), :]
                        far = pltpu.make_async_remote_copy(
                            src_ref=src, dst_ref=dst, send_sem=zsend.at[i], recv_sem=zrecv.at[0],
                            device_id=(y * 2 + cd, x, jnp.int32(zd)), device_id_type=MESH,
                        )
                        if cd == n:

                            @pl.when(z != zd)
                            def _():
                                far.start() if run else far.wait_send()

                            if run:

                                @pl.when(z == zd)
                                def _():
                                    pltpu.make_async_copy(src, dst, zrecv.at[0]).start()
                        else:
                            far.start() if run else far.wait_send()
                        i += 1

    def turn(t):
        for cd in range(2):
            ct[t, cd] = acc[t, cd * TILE : cd * TILE + TILE, :].T

    order = [(0, k) for k in range(10)] + [(1, 0), (1, 1), (0, 10), (0, 11), (1, 2), (1, 3)]
    order += [(0, 12), (0, 13)] + [(1, k) for k in range(4, STEPS)]
    for t, k in order:
        for d in ways:
            got(d, t, k).wait()
            if k < 10:
                sent(d, t, passed(d, k)).start()
            if (t, k) == (0, 7):
                for j in range(EARLY, 4):
                    sent(d, 1, j).start()
        if (t, k) == (0, 2):
            for d in ways:
                lgot(d, 0).wait()
                lsent(d, 2).start()
                lshare(d, 0).start()
        if (t, k) == (0, 5):
            ogot(0, occx, X - 1)
            occy[y] = occx[0] + occx[1] + occx[2] + occx[3]
            for copy in stage_sends[1]:
                copy.start()
        if (t, k) == (0, 7):
            for d in ways:
                lgot(d, 1).wait()
                lshare(d, 1).start()
        if (t, k) == (0, 9):
            ogot(1, occy, Y - 1)
            summed = occy[0]
            for j in range(1, Y):
                summed = summed + occy[j]
            occc[c] = summed
            stage_sends[2][0].start()
        if (t, k) == (1, 3):
            for d in ways:
                lgot(d, 2).wait()
                lshare(d, 2).start()
        if (t, k) == (0, 12):
            for d in ways:
                for j in range(3):
                    lshared(d, j).wait()
            pltpu.make_async_copy(mine, mine, lsibr.at[6]).wait()
            for j in range(2):
                keep_own(j).wait()
            multiply(0, 0, True)
            multiply(0, 1)
            multiply(0, -1)
            ogot(2, occc, 1)
            occz[z] = occc[0] + occc[1]
            agree(1, 2 * len(others), 1)
            for copy in stage_sends[3]:
                copy.start()
        if (t, k) == (0, 13):
            multiply(0, 2)
            multiply(0, -2)
        if (t, k) == (1, 4):
            multiply(0, 3)
            multiply(0, -3)
        if (t, k) == (1, 5):
            multiply(0, 4)
            turn(0)
            scatter(0, True)
        if (t, k) == (1, 8):
            multiply(1, 0, True)
            multiply(1, 1)
        if (t, k) == (1, 9):
            multiply(1, -1)
            multiply(1, 2)
        if (t, k) == (1, 10):
            multiply(1, -2)
        if (t, k) == (1, 11):
            multiply(1, 3)
            multiply(1, -3)
        if (t, k) == (1, 13):
            multiply(1, 4)
            turn(1)
            scatter(1, True)

    ogot(3, occz, Z - 1)
    whole = occz[0]
    for j in range(1, Z):
        whole = whole + occz[j]
    mean = jnp.sum(whole, keepdims=True) / float(ROWS * 2 * Y)
    occ_ref[...] = mean

    for d in ways:
        for t in range(2):
            for k in range(STEPS):
                sent(d, t, k).wait_send()
        for k in range(3):
            lsent(d, k).wait_send()
            lshare(d, k).wait_send()
    for t in range(2):
        swap(t).wait_send()
    share_own.wait_send()
    for copies in stage_sends:
        for copy in copies:
            copy.wait_send()

    pltpu.make_async_copy(zin, zin, zrecv.at[0]).wait()
    square = zin[0]
    for j in range(1, Z):
        square = square + zin[j]
    square = square[:, :ROWS]
    doubled = 2.0 * win_ref[...].astype(jnp.float32) - square
    updated = jnp.where(branchm[...] > 0.5, doubled, square)
    out_ref[...] = jnp.where(keepm[...] > 0.5, updated, 0.0).astype(jnp.bfloat16)
    for t in range(2):
        scatter(t, False)


def shards(row_stripe, column_stripe, window_block, stripe_tiles, column_tiles, keep_tiles, branch):
    bf, f32 = jnp.bfloat16, jnp.float32
    dma = pltpu.SemaphoreType.DMA
    vmem = pl.BlockSpec(memory_space=pltpu.VMEM)
    block, occupancy = pl.pallas_call(
        kernel,
        out_shape=(
            jax.ShapeDtypeStruct((OUT, ROWS), bf),
            jax.ShapeDtypeStruct((1, 1), f32),
        ),
        in_specs=[pl.BlockSpec(memory_space=pl.ANY)] * 7,
        out_specs=(vmem, vmem),
        scratch_shapes=[
            pltpu.VMEM((ROWS, PANEL), bf),
            pltpu.VMEM((SUB, COLS), bf),
            pltpu.VMEM((OUT, ROWS), bf),
            pltpu.VMEM((15, 816), jnp.int32),
            pltpu.VMEM((15, 816), jnp.int32),
            pltpu.VMEM((15, 15), jnp.int32),
            pltpu.VMEM((1, 15), jnp.int32),
            dma((7,)),
            pltpu.VMEM((4, SUB, TILE), bf),
            pltpu.VMEM((2, Y, KWIN, TILE), bf),
            pltpu.VMEM((X, 2 * ROWS_P, PANEL), bf),
            pltpu.VMEM((2, 2 * ROWS_P, TILE), f32),
            pltpu.VMEM((2, 2, TILE, TILE), f32),
            pltpu.VMEM((Z, OUT, TILE), f32),
            pltpu.VMEM((X, 8, TILE), f32),
            pltpu.VMEM((Y, 8, TILE), f32),
            pltpu.VMEM((2, 8, TILE), f32),
            pltpu.VMEM((Z, 8, TILE), f32),
            pltpu.VMEM((OUT, ROWS), f32),
            pltpu.VMEM((OUT, ROWS), f32),
            dma((4 * STEPS,)), dma((4 * STEPS,)), pltpu.SemaphoreType.REGULAR((2,)),
            dma((2,)), dma((2,)), dma((2,)),
            dma((6,)), dma((6,)), dma((7,)), dma((7,)),
            dma((16,)), dma((1,)),
            dma((22,)), dma((4,)),
        ],
        compiler_params=pltpu.CompilerParams(
            collective_id=0, has_side_effects=True, vmem_limit_bytes=56 * 2**20
        ),
        name="square",
    )(
        row_stripe[:, 0, :], column_stripe[0], window_block.T, stripe_tiles, column_tiles.T,
        keep_tiles, branch[None, :],
    )
    return block.T, occupancy[0, 0]


def solution(mesh):
    return jax.shard_map(
        shards,
        mesh=mesh,
        in_specs=(
            P("row", "depth", "col"),
            P("depth", "row", "col"),
            P("row", ("col", "depth")),
            P(),
            P(),
            P(),
            P(),
        ),
        out_specs=(P("row", ("col", "depth")), P()),
        check_vma=False,
    )
```

```python
import functools

import jax
import jax.numpy as jnp
from jax import lax
from jax.experimental import pallas as pl
from jax.experimental.pallas import tpu as pltpu
from jax.sharding import PartitionSpec as P

TILE = 128
MESH = pl.DeviceIdType.MESH
X, Y, Z = 4, 8, 12
ROWS = 120
ROWS_P = 128
PANEL = 2176
SUB = 544
COLS = 480
OUT = 40
KWIN = 1152
PART = 272
EARLY = 3
STEPS = 14
LAST = COLS - 3 * TILE
SPARE = TILE - LAST


def segments(tile):
    found = []
    for z in range(Z):
        low = max(tile * TILE, z * OUT)
        high = min(tile * TILE + TILE, COLS, z * OUT + OUT)
        if low < high:
            found.append((z, low - tile * TILE, high - low, low - z * OUT))
    return found


def hops(d, t, core):
    if t == 1 and core == 1:
        first = [2 * PART, 0, PART]
        third = first if d > 0 else [PART, 2 * PART, 0]
        fourth = first[:2] if d > 0 else [PART]
    else:
        own = [core * SUB, core * SUB + PART]
        other = [SUB - core * SUB, SUB - core * SUB + PART]
        first = own + other
        third = first if d > 0 else other + own
        fourth = own if d > 0 else other
    return [(h + 1, row) for h, rows in enumerate((first, first, third, fourth)) for row in rows]


def one_hot(hit):
    return jnp.where(hit, 1.0, 0.0).astype(jnp.bfloat16)


def dot(a, b):
    return jnp.dot(a, b, preferred_element_type=jnp.float32)


def dot_t(a, b):
    dims = (((1,), (1,)), ((), ()))
    return lax.dot_general(a, b, dims, preferred_element_type=jnp.float32)


def kernel(
    row_in, col_in, win_in, stripe_in, ctab_in, keep_in, branch_in,
    out_ref, occ_ref,
    row_ref, col_ref, win_ref, stripe_ref, ctab_ref, keep_ref, branch_ref, in_sem,
    rm, rb, lg, acc, ct, zin, occx, occy, occc, occz, keepm, branchm, um,
    rsend, rrecv, go, dsend, drecv, own_sem, lsend, lrecv, lsibs, lsibr, zsend, zrecv, osend, orecv,
):
    r = lax.axis_index("row")
    x = lax.axis_index("col")
    z = lax.axis_index("depth")
    y = r // 2
    c = r % 2

    def ydev(d):
        return (((y + d) % Y) * 2 + c, x, z)

    def xdev(d):
        return (r, (x + d) % X, z)

    sib = (y * 2 + (1 - c), x, z)

    arrays = [
        (ctab_in, ctab_ref), (col_in, col_ref), (stripe_in, stripe_ref), (row_in, row_ref),
        (keep_in, keep_ref), (branch_in, branch_ref), (win_in, win_ref),
    ]
    loads = [pltpu.make_async_copy(a, b, in_sem.at[i]) for i, (a, b) in enumerate(arrays)]
    for load in loads:
        load.start()

    barrier = pltpu.get_barrier_semaphore()
    plane = [((y + d) % Y * 2, x, z) for d in range(1, Y)] + [(y * 2, (x + d) % X, z) for d in range(1, X)]
    others = [(y * 2 + 1, x, (z + d) % Z) for d in range(1, Z)]
    for peer in plane:
        pl.semaphore_signal(barrier, inc=1, device_id=peer, device_id_type=MESH)

    @pl.when(c == 1)
    def _():
        pl.semaphore_signal(barrier, inc=1, device_id=sib, device_id_type=MESH)

    def agree(counter, count, i):
        @pl.when(c == counter)
        def _():
            pl.semaphore_wait(barrier, count)
            pl.semaphore_signal(go.at[i], inc=1, device_id=sib, device_id_type=MESH)

        @pl.when(c != counter)
        def _():
            pl.semaphore_wait(go.at[i], 1)

    for t in range(2):
        for yy in range(Y):
            low = 0 if yy % 2 else 2 * SUB
            rb[t, yy, low : low + 64, :] = jnp.zeros((64, TILE), jnp.bfloat16)

    first = z * 68 + (r * SUB) // TILE
    skew = (r * SUB) % TILE
    loads[0].wait()
    ctab = one_hot(ctab_ref[...] > 0)
    pick = one_hot(
        lax.broadcasted_iota(jnp.int32, (16, 816), 1)
        == lax.broadcasted_iota(jnp.int32, (16, 816), 0) + first
    )
    picked = dot_t(pick, ctab).astype(jnp.bfloat16)
    spread = one_hot(
        lax.broadcasted_iota(jnp.int32, (15, 512), 0)
        == (lax.broadcasted_iota(jnp.int32, (15, 512), 1) + x * COLS) // TILE
    )
    by_col = dot(picked, spread).astype(jnp.bfloat16)
    band = one_hot(
        lax.broadcasted_iota(jnp.int32, (SUB, 16), 1)
        == (lax.broadcasted_iota(jnp.int32, (SUB, 16), 0) + skew) // TILE
    )

    def masked(tile):
        wide = min(TILE, COLS - tile * TILE)
        if wide < TILE:
            rm[tile] = jnp.zeros((SUB, TILE), jnp.bfloat16)
        mask = dot(band, by_col[:, tile * TILE : tile * TILE + wide]).astype(jnp.bfloat16)
        rm[tile, :, 0:wide] = col_ref[:, tile * TILE : tile * TILE + wide] * mask

    loads[1].wait()
    for n in range(2):

        @pl.when(c == n)
        def _():
            masked(n)

    agree(0, 2 * len(plane) + 1, 0)

    def off(yy, cc):
        return pl.multiple_of((yy % 2) * 64 + cc * SUB, 32)

    def piece(t, yy, cc):
        return rb.at[t, yy, pl.ds(off(yy, cc), SUB), :]

    def block(t, yy, row):
        start = pl.multiple_of((yy % 2) * 64 + row, 16)
        return rb.at[t, yy, pl.ds(start, PART), :]

    def sent(d, t, k, row, hop, here=None):
        there = block(t, (y - d * (hop - 1) + Y) % Y, row)
        i = ((0 if d > 0 else 2) + t) * STEPS + k
        return pltpu.make_async_remote_copy(
            src_ref=there if here is None else here, dst_ref=there, send_sem=rsend.at[i],
            recv_sem=rrecv.at[i], device_id=ydev(d % Y), device_id_type=MESH,
        )

    def got(d, t, k, row, hop):
        here = block(t, (y - d * hop + Y) % Y, row)
        i = ((0 if d > 0 else 2) + t) * STEPS + k
        return pltpu.make_async_copy(here, here, rrecv.at[i])

    def first_hop(d, t, k):
        part = (k % 2) * PART
        if k < 2:
            return sent(d, t, k, c * SUB + part, 1, rm.at[2 * t + c, part : part + PART, :])
        return sent(d, t, k, (1 - c) * SUB + part, 1)

    ways = (1, -1)
    for k in range(2):
        for d in ways:
            first_hop(d, 0, k).start()

    def swap(t):
        return pltpu.make_async_remote_copy(
            src_ref=rm.at[2 * t + 1 - c], dst_ref=piece(t, y, c),
            send_sem=dsend.at[t], recv_sem=drecv.at[t], device_id=sib, device_id_type=MESH,
        )

    def keep_own(t):
        return pltpu.make_async_copy(rm.at[2 * t + c], piece(t, y, c), own_sem.at[t])

    def swapped(t):
        here = piece(t, y, 1 - c)
        return pltpu.make_async_copy(here, here, drecv.at[t])

    for n in range(2):

        @pl.when(c != n)
        def _():
            masked(n)

    swap(0).start()
    keep_own(0).start()
    for peer in others:
        pl.semaphore_signal(barrier, inc=1, device_id=peer, device_id_type=MESH)
    masked(2)
    masked(3)
    swap(1).start()

    @pl.when(c == 0)
    def _():
        keep_own(1).start()


    loads[2].wait()
    loads[3].wait()
    stab = one_hot(stripe_ref[...] > 0)
    base = z * 68 + x * 17
    shift = one_hot(
        lax.broadcasted_iota(jnp.int32, (816, TILE), 0)
        == lax.broadcasted_iota(jnp.int32, (816, TILE), 1) + base
    )
    narrow = dot(stab, shift).astype(jnp.bfloat16)
    rows_in = one_hot(
        lax.broadcasted_iota(jnp.int32, (ROWS, 15), 1)
        == (lax.broadcasted_iota(jnp.int32, (ROWS, 15), 0) + r * ROWS) // TILE
    )
    lmask = dot(rows_in, narrow)
    total = jnp.zeros((8, TILE), jnp.float32)
    myrow = pl.multiple_of(c * ROWS_P, ROWS_P)
    for k in range(17):
        part = row_ref[:, k * TILE : k * TILE + TILE].astype(jnp.float32)
        part = part * lmask[:, k : k + 1]
        total = total + jnp.sum((part * part).reshape(15, 8, TILE), axis=0)
        whole = jnp.concatenate([part, jnp.zeros((8, TILE), jnp.float32)], axis=0)
        lg[x, pl.ds(myrow, ROWS_P), k * TILE : k * TILE + TILE] = whole.astype(jnp.bfloat16)
    occx[x] = total

    def half(panel, low):
        return lg.at[panel, pl.ds(pl.multiple_of(myrow + low, 64), 64), :]

    def lowrow(d, k):
        ahead = 0 if d > 0 else 64
        return 64 - ahead if k == 1 else ahead

    def lindex(d, k):
        return (0 if d > 0 else 3) + k

    def lsent(d, k):
        panel = (x - d + X) % X if k == 2 else x
        ref = half(panel, lowrow(d, k))
        return pltpu.make_async_remote_copy(
            src_ref=ref, dst_ref=ref, send_sem=lsend.at[lindex(d, k)],
            recv_sem=lrecv.at[lindex(d, k)], device_id=xdev(d % X), device_id_type=MESH,
        )

    def lpart(d, k):
        panel = (x - (2 * d if k == 2 else d) + X) % X
        return half(panel, lowrow(d, k))

    def lgot(d, k):
        here = lpart(d, k)
        return pltpu.make_async_copy(here, here, lrecv.at[lindex(d, k)])

    def lshare(d, k):
        ref = lpart(d, k)
        return pltpu.make_async_remote_copy(
            src_ref=ref, dst_ref=ref, send_sem=lsibs.at[lindex(d, k)],
            recv_sem=lsibr.at[lindex(d, k)], device_id=sib, device_id_type=MESH,
        )

    otherrow = pl.multiple_of((1 - c) * ROWS_P, ROWS_P)

    def lshared(d, k):
        panel = (x - (2 * d if k == 2 else d) + X) % X
        here = lg.at[panel, pl.ds(pl.multiple_of(otherrow + lowrow(d, k), 64), 64), :]
        return pltpu.make_async_copy(here, here, lsibr.at[lindex(d, k)])

    mine = lg.at[x, pl.ds(myrow, ROWS_P), :]
    share_own = pltpu.make_async_remote_copy(
        src_ref=mine, dst_ref=mine, send_sem=lsibs.at[6], recv_sem=lsibr.at[6],
        device_id=sib, device_id_type=MESH,
    )

    for k in range(2):
        for d in ways:
            lsent(d, k).start()
    share_own.start()

    swapped(0).wait()
    for k in range(2, 4):
        for d in ways:
            first_hop(d, 0, k).start()

    lane_in = lax.broadcasted_iota(jnp.int32, (TILE, TILE), 0)
    lane_out = lax.broadcasted_iota(jnp.int32, (TILE, TILE), 1)
    for g in range(3):
        um[g] = one_hot((lane_in >= LAST) & (lane_in - LAST + g * SPARE == lane_out))

    swapped(1).wait()

    @pl.when(c == 0)
    def _():
        for k in range(EARLY):
            for d in ways:
                first_hop(d, 1, k).start()

    @pl.when(c == 1)
    def _():
        fourth = rm[3, PART:SUB, :]
        block(1, y, 3 * PART)[...] = fourth
        for g in (2, 0, 1):
            main = rm[3, 0:PART, :] if g == 2 else block(1, y, g * PART)[...]
            extra = dot_t(fourth, um[g])
            block(1, y, g * PART)[...] = (main.astype(jnp.float32) + extra).astype(jnp.bfloat16)
        for k in range(min(EARLY, 3)):
            for d in ways:
                sent(d, 1, k, *hops(d, 1, 1)[k][::-1]).start()

    def osent(stage, i, buf, slot, device):
        return pltpu.make_async_remote_copy(
            src_ref=buf.at[slot], dst_ref=buf.at[slot], send_sem=osend.at[i],
            recv_sem=orecv.at[stage], device_id=device, device_id_type=MESH,
        )

    stage_sends = [
        [osent(0, d - 1, occx, x, xdev(d)) for d in range(1, X)],
        [osent(1, 2 + d, occy, y, ydev(d)) for d in range(1, Y)],
        [osent(2, 10, occc, c, sib)],
        [osent(3, 10 + d, occz, z, (r, x, (z + d) % Z)) for d in range(1, Z)],
    ]

    def ogot(stage, buf, n):
        here = buf.at[pl.ds(0, n)]
        pltpu.make_async_copy(here, here, orecv.at[stage]).wait()

    for copy in stage_sends[0]:
        copy.start()

    for load in loads[4:]:
        load.wait()
    tabk = one_hot(keep_ref[...] > 0)
    cols_in = one_hot(
        lax.broadcasted_iota(jnp.int32, (OUT, 15), 1)
        == (lax.broadcasted_iota(jnp.int32, (OUT, 15), 0) + x * COLS + z * OUT) // TILE
    )
    across = one_hot(
        lax.broadcasted_iota(jnp.int32, (15, ROWS), 0)
        == (lax.broadcasted_iota(jnp.int32, (15, ROWS), 1) + r * ROWS) // TILE
    )
    keepm[...] = dot(dot_t(cols_in, tabk).astype(jnp.bfloat16), across)
    flag = jnp.broadcast_to(one_hot(branch_ref[...] > 0), (OUT, 15))
    branchm[...] = dot(flag, across)

    def multiply(n, t, step, begin=False):
        yy = (y + step + Y) % Y
        if t == 1 and n == 1 and step != 0:
            fourth = dot(block(1, yy, 0)[...], um[0])
            for g in (1, 2):
                fourth = fourth + dot(block(1, yy, g * PART)[...], um[g])
            block(1, yy, 3 * PART)[...] = fourth.astype(jnp.bfloat16)
        window = pl.multiple_of((yy % 2) * 1024, 1024)
        product = dot(lg[yy // 2, :, pl.ds(window, KWIN)], rb[t, yy])
        if begin:
            acc[t] = product
        else:
            acc[t] += product

    def scatter(t, run):
        for n in range(2):

            @pl.when(c == n)
            def _():
                i = t * 8
                for zd, low, rows, at in segments(2 * t + n):
                    for cd in range(2):
                        src = ct.at[t, cd, pl.ds(low, rows), :]
                        dst = zin.at[z, pl.ds(at, rows), :]
                        far = pltpu.make_async_remote_copy(
                            src_ref=src, dst_ref=dst, send_sem=zsend.at[i], recv_sem=zrecv.at[0],
                            device_id=(y * 2 + cd, x, jnp.int32(zd)), device_id_type=MESH,
                        )
                        if cd == n:

                            @pl.when(z != zd)
                            def _():
                                far.start() if run else far.wait_send()

                            if run:

                                @pl.when(z == zd)
                                def _():
                                    pltpu.make_async_copy(src, dst, zrecv.at[0]).start()
                        else:
                            far.start() if run else far.wait_send()
                        i += 1

    def turn(t):
        for cd in range(2):
            ct[t, cd] = acc[t, cd * TILE : cd * TILE + TILE, :].T

    points = (
        dict(
            la=(0, 2), o1=(0, 5), lb=(0, 7), o2=(0, 9), lf=(1, 3), m0a=(0, 12), m0b=(0, 13), m0c=(1, 4),
            m0d=(1, 5), m1a=(1, 8), m1b=(1, 9), m1c=(1, 10), m1d=(1, 11), end=(1, 13),
        ),
        dict(
            la=(0, 2), o1=(0, 5), lb=(0, 7), o2=(0, 9), lf=(1, 2), m0a=(0, 12), m0b=(0, 13), m0c=(1, 3),
            m0d=(1, 4), m1a=(1, 6), m1b=(1, 7), m1c=(1, 8), m1d=(1, 9), end=(1, 10),
        ),
    )

    def ring(n):
        at = points[n]
        pieces = {(d, t): hops(d, t, n) for d in ways for t in range(2)}
        order = [(0, k) for k in range(10)] + [(1, 0), (1, 1), (0, 10), (0, 11)]
        order += ([(1, 2), (1, 3)] if n == 0 else [(1, 2)]) + [(0, 12), (0, 13)]
        order += [(1, k) for k in (range(4, 14) if n == 0 else range(3, 11))]
        for t, k in order:
            for d in ways:
                mine_d = pieces[d, t]
                if k < len(mine_d):
                    hop, row = mine_d[k]
                    got(d, t, k, row, hop).wait()
                    if (hop + 1, row) in mine_d:
                        sent(d, t, mine_d.index((hop + 1, row)), row, hop + 1).start()
                if (t, k) == (0, 7):
                    for j in range(EARLY, 4 - n):
                        if n == 0:
                            first_hop(d, 1, j).start()
                        else:
                            sent(d, 1, j, *pieces[d, 1][j][::-1]).start()
            if (t, k) == at["la"]:
                for d in ways:
                    lgot(d, 0).wait()
                    lsent(d, 2).start()
                    lshare(d, 0).start()
            if (t, k) == at["o1"]:
                ogot(0, occx, X - 1)
                occy[y] = occx[0] + occx[1] + occx[2] + occx[3]
                for copy in stage_sends[1]:
                    copy.start()
            if (t, k) == at["lb"]:
                for d in ways:
                    lgot(d, 1).wait()
                    lshare(d, 1).start()
            if (t, k) == at["o2"]:
                ogot(1, occy, Y - 1)
                summed = occy[0]
                for j in range(1, Y):
                    summed = summed + occy[j]
                occc[c] = summed
                stage_sends[2][0].start()
            if (t, k) == at["lf"]:
                for d in ways:
                    lgot(d, 2).wait()
                    lshare(d, 2).start()
            if (t, k) == at["m0a"]:
                for d in ways:
                    for j in range(3):
                        lshared(d, j).wait()
                pltpu.make_async_copy(mine, mine, lsibr.at[6]).wait()
                for j in range(2 - n):
                    keep_own(j).wait()
                multiply(n, 0, 0, True)
                multiply(n, 0, 1)
                multiply(n, 0, -1)
                ogot(2, occc, 1)
                occz[z] = occc[0] + occc[1]
                agree(1, 2 * len(others), 1)
                for copy in stage_sends[3]:
                    copy.start()
            if (t, k) == at["m0b"]:
                multiply(n, 0, 2)
                multiply(n, 0, -2)
            if (t, k) == at["m0c"]:
                multiply(n, 0, 3)
                multiply(n, 0, -3)
            if (t, k) == at["m0d"]:
                multiply(n, 0, 4)
                turn(0)
                scatter(0, True)
            if (t, k) == at["m1a"]:
                multiply(n, 1, 0, True)
                multiply(n, 1, 1)
            if (t, k) == at["m1b"]:
                multiply(n, 1, -1)
                multiply(n, 1, 2)
            if (t, k) == at["m1c"]:
                multiply(n, 1, -2)
            if (t, k) == at["m1d"]:
                multiply(n, 1, 3)
                multiply(n, 1, -3)
            if (t, k) == at["end"]:
                multiply(n, 1, 4)
                turn(1)
                scatter(1, True)
        for (d, t), listed in pieces.items():
            for k, (hop, row) in enumerate(listed):
                sent(d, t, k, row, hop).wait_send()

    for n in range(2):

        @pl.when(c == n)
        def _():
            ring(n)

    ogot(3, occz, Z - 1)
    whole = occz[0]
    for j in range(1, Z):
        whole = whole + occz[j]
    mean = jnp.sum(whole, keepdims=True) / float(ROWS * 2 * Y)
    occ_ref[...] = mean

    for d in ways:
        for k in range(3):
            lsent(d, k).wait_send()
            lshare(d, k).wait_send()
    for t in range(2):
        swap(t).wait_send()
    share_own.wait_send()
    for copies in stage_sends:
        for copy in copies:
            copy.wait_send()

    pltpu.make_async_copy(zin, zin, zrecv.at[0]).wait()
    square = zin[0]
    for j in range(1, Z):
        square = square + zin[j]
    square = square[:, :ROWS]
    doubled = 2.0 * win_ref[...].astype(jnp.float32) - square
    updated = jnp.where(branchm[...] > 0.5, doubled, square)
    out_ref[...] = jnp.where(keepm[...] > 0.5, updated, 0.0).astype(jnp.bfloat16)
    for t in range(2):
        scatter(t, False)


def shards(row_stripe, column_stripe, window_block, stripe_tiles, column_tiles, keep_tiles, branch):
    bf, f32 = jnp.bfloat16, jnp.float32
    dma = pltpu.SemaphoreType.DMA
    vmem = pl.BlockSpec(memory_space=pltpu.VMEM)
    block, occupancy = pl.pallas_call(
        kernel,
        out_shape=(
            jax.ShapeDtypeStruct((OUT, ROWS), bf),
            jax.ShapeDtypeStruct((1, 1), f32),
        ),
        in_specs=[pl.BlockSpec(memory_space=pl.ANY)] * 7,
        out_specs=(vmem, vmem),
        scratch_shapes=[
            pltpu.VMEM((ROWS, PANEL), bf),
            pltpu.VMEM((SUB, COLS), bf),
            pltpu.VMEM((OUT, ROWS), bf),
            pltpu.VMEM((15, 816), jnp.int32),
            pltpu.VMEM((15, 816), jnp.int32),
            pltpu.VMEM((15, 15), jnp.int32),
            pltpu.VMEM((1, 15), jnp.int32),
            dma((7,)),
            pltpu.VMEM((4, SUB, TILE), bf),
            pltpu.VMEM((2, Y, KWIN, TILE), bf),
            pltpu.VMEM((X, 2 * ROWS_P, PANEL), bf),
            pltpu.VMEM((2, 2 * ROWS_P, TILE), f32),
            pltpu.VMEM((2, 2, TILE, TILE), f32),
            pltpu.VMEM((Z, OUT, TILE), f32),
            pltpu.VMEM((X, 8, TILE), f32),
            pltpu.VMEM((Y, 8, TILE), f32),
            pltpu.VMEM((2, 8, TILE), f32),
            pltpu.VMEM((Z, 8, TILE), f32),
            pltpu.VMEM((OUT, ROWS), f32),
            pltpu.VMEM((OUT, ROWS), f32),
            pltpu.VMEM((3, TILE, TILE), bf),
            dma((4 * STEPS,)), dma((4 * STEPS,)), pltpu.SemaphoreType.REGULAR((2,)),
            dma((2,)), dma((2,)), dma((2,)),
            dma((6,)), dma((6,)), dma((7,)), dma((7,)),
            dma((16,)), dma((1,)),
            dma((22,)), dma((4,)),
        ],
        compiler_params=pltpu.CompilerParams(
            collective_id=0, has_side_effects=True, vmem_limit_bytes=56 * 2**20
        ),
        name="square",
    )(
        row_stripe[:, 0, :], column_stripe[0], window_block.T, stripe_tiles, column_tiles.T,
        keep_tiles, branch[None, :],
    )
    return block.T, occupancy[0, 0]


def solution(mesh):
    return jax.shard_map(
        shards,
        mesh=mesh,
        in_specs=(
            P("row", "depth", "col"),
            P("depth", "row", "col"),
            P("row", ("col", "depth")),
            P(),
            P(),
            P(),
            P(),
        ),
        out_specs=(P("row", ("col", "depth")), P()),
        check_vma=False,
    )
```

```python
import functools

import jax
import jax.numpy as jnp
from jax import lax
from jax.experimental import pallas as pl
from jax.experimental.pallas import tpu as pltpu
from jax.sharding import PartitionSpec as P

TILE = 128
MESH = pl.DeviceIdType.MESH
X, Y, Z = 4, 8, 12
ROWS = 120
ROWS_P = 128
PANEL = 2176
SUB = 544
COLS = 480
OUT = 40
KWIN = 1152
PART = 272
EARLY = 2
STEPS = 14
LAST = COLS - 3 * TILE
SPARE = TILE - LAST


def segments(tile):
    found = []
    for z in range(Z):
        low = max(tile * TILE, z * OUT)
        high = min(tile * TILE + TILE, COLS, z * OUT + OUT)
        if low < high:
            found.append((z, low - tile * TILE, high - low, low - z * OUT))
    return found


def hops(d, t, core):
    if t == 1 and core == 1:
        first = [2 * PART, 0, PART]
        third = first if d > 0 else [PART, 2 * PART, 0]
        fourth = first[:2] if d > 0 else [PART]
    else:
        own = [core * SUB, core * SUB + PART]
        other = [SUB - core * SUB, SUB - core * SUB + PART]
        first = own + other
        third = first if d > 0 else other + own
        fourth = own if d > 0 else other
    return [(h + 1, row) for h, rows in enumerate((first, first, third, fourth)) for row in rows]


def one_hot(hit):
    return jnp.where(hit, 1.0, 0.0).astype(jnp.bfloat16)


def dot(a, b):
    return jnp.dot(a, b, preferred_element_type=jnp.float32)


def dot_t(a, b):
    dims = (((1,), (1,)), ((), ()))
    return lax.dot_general(a, b, dims, preferred_element_type=jnp.float32)


def kernel(
    row_in, col_in, win_in, stripe_in, ctab_in, keep_in, branch_in,
    out, occ_out,
    row_ref, col_ref, win_ref, stripe_ref, ctab_ref, keep_ref, branch_ref, in_sem, out_ref, occ_ref, out_sem,
    rm, rb, lg, acc, ct, zin, occx, occy, occc, occz, keepm, branchm, um,
    rsend, rrecv, go, dsend, drecv, own_sem, lsend, lrecv, lsibs, lsibr, zsend, zrecv, osend, orecv,
):
    r = lax.axis_index("row")
    x = lax.axis_index("col")
    z = lax.axis_index("depth")
    y = r // 2
    c = r % 2

    def ydev(d):
        return (((y + d) % Y) * 2 + c, x, z)

    def xdev(d):
        return (r, (x + d) % X, z)

    sib = (y * 2 + (1 - c), x, z)

    arrays = [
        (ctab_in, ctab_ref), (col_in, col_ref), (stripe_in, stripe_ref), (row_in, row_ref),
        (keep_in, keep_ref), (branch_in, branch_ref), (win_in, win_ref),
    ]
    loads = [pltpu.make_async_copy(a, b, in_sem.at[i]) for i, (a, b) in enumerate(arrays)]
    for load in loads:
        load.start()

    barrier = pltpu.get_barrier_semaphore()
    plane = [((y + d) % Y * 2, x, z) for d in range(1, Y)] + [(y * 2, (x + d) % X, z) for d in range(1, X)]
    others = [(y * 2 + 1, x, (z + d) % Z) for d in range(1, Z)]
    for peer in plane:
        pl.semaphore_signal(barrier, inc=1, device_id=peer, device_id_type=MESH)

    @pl.when(c == 1)
    def _():
        pl.semaphore_signal(barrier, inc=1, device_id=sib, device_id_type=MESH)

    def agree(counter, count, i):
        @pl.when(c == counter)
        def _():
            pl.semaphore_wait(barrier, count)
            pl.semaphore_signal(go.at[i], inc=1, device_id=sib, device_id_type=MESH)

        @pl.when(c != counter)
        def _():
            pl.semaphore_wait(go.at[i], 1)

    for t in range(2):
        for yy in range(Y):
            low = 0 if yy % 2 else 2 * SUB
            rb[t, yy, low : low + 64, :] = jnp.zeros((64, TILE), jnp.bfloat16)

    first = z * 68 + (r * SUB) // TILE
    skew = (r * SUB) % TILE
    loads[0].wait()
    ctab = one_hot(ctab_ref[...] > 0)
    pick = one_hot(
        lax.broadcasted_iota(jnp.int32, (16, 816), 1)
        == lax.broadcasted_iota(jnp.int32, (16, 816), 0) + first
    )
    picked = dot_t(pick, ctab).astype(jnp.bfloat16)
    spread = one_hot(
        lax.broadcasted_iota(jnp.int32, (15, 512), 0)
        == (lax.broadcasted_iota(jnp.int32, (15, 512), 1) + x * COLS) // TILE
    )
    by_col = dot(picked, spread).astype(jnp.bfloat16)
    band = one_hot(
        lax.broadcasted_iota(jnp.int32, (SUB, 16), 1)
        == (lax.broadcasted_iota(jnp.int32, (SUB, 16), 0) + skew) // TILE
    )

    def masked(tile):
        wide = min(TILE, COLS - tile * TILE)
        if wide < TILE:
            rm[tile] = jnp.zeros((SUB, TILE), jnp.bfloat16)
        mask = dot(band, by_col[:, tile * TILE : tile * TILE + wide]).astype(jnp.bfloat16)
        rm[tile, :, 0:wide] = col_ref[:, tile * TILE : tile * TILE + wide] * mask

    loads[1].wait()
    for n in range(2):

        @pl.when(c == n)
        def _():
            masked(n)

    agree(0, 2 * len(plane) + 1, 0)

    def off(yy, cc):
        return pl.multiple_of((yy % 2) * 64 + cc * SUB, 32)

    def piece(t, yy, cc):
        return rb.at[t, yy, pl.ds(off(yy, cc), SUB), :]

    def block(t, yy, row):
        start = pl.multiple_of((yy % 2) * 64 + row, 16)
        return rb.at[t, yy, pl.ds(start, PART), :]

    def sent(d, t, k, row, hop, here=None):
        there = block(t, (y - d * (hop - 1) + Y) % Y, row)
        i = ((0 if d > 0 else 2) + t) * STEPS + k
        return pltpu.make_async_remote_copy(
            src_ref=there if here is None else here, dst_ref=there, send_sem=rsend.at[i],
            recv_sem=rrecv.at[i], device_id=ydev(d % Y), device_id_type=MESH,
        )

    def got(d, t, k, row, hop):
        here = block(t, (y - d * hop + Y) % Y, row)
        i = ((0 if d > 0 else 2) + t) * STEPS + k
        return pltpu.make_async_copy(here, here, rrecv.at[i])

    def first_hop(d, t, k):
        part = (k % 2) * PART
        if k < 2:
            return sent(d, t, k, c * SUB + part, 1, rm.at[2 * t + c, part : part + PART, :])
        return sent(d, t, k, (1 - c) * SUB + part, 1)

    ways = (1, -1)
    for k in range(2):
        for d in ways:
            first_hop(d, 0, k).start()

    def swap(t):
        return pltpu.make_async_remote_copy(
            src_ref=rm.at[2 * t + 1 - c], dst_ref=piece(t, y, c),
            send_sem=dsend.at[t], recv_sem=drecv.at[t], device_id=sib, device_id_type=MESH,
        )

    def keep_own(t):
        return pltpu.make_async_copy(rm.at[2 * t + c], piece(t, y, c), own_sem.at[t])

    def swapped(t):
        here = piece(t, y, 1 - c)
        return pltpu.make_async_copy(here, here, drecv.at[t])

    for n in range(2):

        @pl.when(c != n)
        def _():
            masked(n)

    swap(0).start()
    keep_own(0).start()
    for peer in others:
        pl.semaphore_signal(barrier, inc=1, device_id=peer, device_id_type=MESH)
    masked(2)
    masked(3)
    swap(1).start()

    @pl.when(c == 0)
    def _():
        keep_own(1).start()


    loads[2].wait()
    loads[3].wait()
    stab = one_hot(stripe_ref[...] > 0)
    base = z * 68 + x * 17
    shift = one_hot(
        lax.broadcasted_iota(jnp.int32, (816, TILE), 0)
        == lax.broadcasted_iota(jnp.int32, (816, TILE), 1) + base
    )
    narrow = dot(stab, shift).astype(jnp.bfloat16)
    rows_in = one_hot(
        lax.broadcasted_iota(jnp.int32, (ROWS, 15), 1)
        == (lax.broadcasted_iota(jnp.int32, (ROWS, 15), 0) + r * ROWS) // TILE
    )
    lmask = dot(rows_in, narrow)
    total = jnp.zeros((8, TILE), jnp.float32)
    myrow = pl.multiple_of(c * ROWS_P, ROWS_P)
    for k in range(17):
        part = row_ref[:, k * TILE : k * TILE + TILE].astype(jnp.float32)
        part = part * lmask[:, k : k + 1]
        total = total + jnp.sum((part * part).reshape(15, 8, TILE), axis=0)
        whole = jnp.concatenate([part, jnp.zeros((8, TILE), jnp.float32)], axis=0)
        lg[x, pl.ds(myrow, ROWS_P), k * TILE : k * TILE + TILE] = whole.astype(jnp.bfloat16)
    occx[x] = total

    def half(panel, low):
        return lg.at[panel, pl.ds(pl.multiple_of(myrow + low, 64), 64), :]

    def lowrow(d, k):
        ahead = 0 if d > 0 else 64
        return 64 - ahead if k == 1 else ahead

    def lindex(d, k):
        return (0 if d > 0 else 3) + k

    def lsent(d, k):
        panel = (x - d + X) % X if k == 2 else x
        ref = half(panel, lowrow(d, k))
        return pltpu.make_async_remote_copy(
            src_ref=ref, dst_ref=ref, send_sem=lsend.at[lindex(d, k)],
            recv_sem=lrecv.at[lindex(d, k)], device_id=xdev(d % X), device_id_type=MESH,
        )

    def lpart(d, k):
        panel = (x - (2 * d if k == 2 else d) + X) % X
        return half(panel, lowrow(d, k))

    def lgot(d, k):
        here = lpart(d, k)
        return pltpu.make_async_copy(here, here, lrecv.at[lindex(d, k)])

    def lshare(d, k):
        ref = lpart(d, k)
        return pltpu.make_async_remote_copy(
            src_ref=ref, dst_ref=ref, send_sem=lsibs.at[lindex(d, k)],
            recv_sem=lsibr.at[lindex(d, k)], device_id=sib, device_id_type=MESH,
        )

    otherrow = pl.multiple_of((1 - c) * ROWS_P, ROWS_P)

    def lshared(d, k):
        panel = (x - (2 * d if k == 2 else d) + X) % X
        here = lg.at[panel, pl.ds(pl.multiple_of(otherrow + lowrow(d, k), 64), 64), :]
        return pltpu.make_async_copy(here, here, lsibr.at[lindex(d, k)])

    mine = lg.at[x, pl.ds(myrow, ROWS_P), :]
    share_own = pltpu.make_async_remote_copy(
        src_ref=mine, dst_ref=mine, send_sem=lsibs.at[6], recv_sem=lsibr.at[6],
        device_id=sib, device_id_type=MESH,
    )

    for k in range(2):
        for d in ways:
            lsent(d, k).start()
    share_own.start()

    swapped(0).wait()
    for k in range(2, 4):
        for d in ways:
            first_hop(d, 0, k).start()

    lane_in = lax.broadcasted_iota(jnp.int32, (TILE, TILE), 0)
    lane_out = lax.broadcasted_iota(jnp.int32, (TILE, TILE), 1)
    for g in range(3):
        um[g] = one_hot((lane_in >= LAST) & (lane_in - LAST + g * SPARE == lane_out))

    swapped(1).wait()

    @pl.when(c == 0)
    def _():
        for k in range(EARLY):
            for d in ways:
                first_hop(d, 1, k).start()

    @pl.when(c == 1)
    def _():
        fourth = rm[3, PART:SUB, :]
        block(1, y, 3 * PART)[...] = fourth
        for g in (2, 0, 1):
            main = rm[3, 0:PART, :] if g == 2 else block(1, y, g * PART)[...]
            extra = dot_t(fourth, um[g])
            block(1, y, g * PART)[...] = (main.astype(jnp.float32) + extra).astype(jnp.bfloat16)
        for k in range(min(EARLY, 3)):
            for d in ways:
                sent(d, 1, k, *hops(d, 1, 1)[k][::-1]).start()

    def osent(stage, i, buf, slot, device):
        return pltpu.make_async_remote_copy(
            src_ref=buf.at[slot], dst_ref=buf.at[slot], send_sem=osend.at[i],
            recv_sem=orecv.at[stage], device_id=device, device_id_type=MESH,
        )

    stage_sends = [
        [osent(0, d - 1, occx, x, xdev(d)) for d in range(1, X)],
        [osent(1, 2 + d, occy, y, ydev(d)) for d in range(1, Y)],
        [osent(2, 10, occc, c, sib)],
        [osent(3, 10 + d, occz, z, (r, x, (z + d) % Z)) for d in range(1, Z)],
    ]

    def ogot(stage, buf, n):
        here = buf.at[pl.ds(0, n)]
        pltpu.make_async_copy(here, here, orecv.at[stage]).wait()

    for copy in stage_sends[0]:
        copy.start()

    for load in loads[4:]:
        load.wait()
    tabk = one_hot(keep_ref[...] > 0)
    cols_in = one_hot(
        lax.broadcasted_iota(jnp.int32, (OUT, 15), 1)
        == (lax.broadcasted_iota(jnp.int32, (OUT, 15), 0) + x * COLS + z * OUT) // TILE
    )
    across = one_hot(
        lax.broadcasted_iota(jnp.int32, (15, ROWS), 0)
        == (lax.broadcasted_iota(jnp.int32, (15, ROWS), 1) + r * ROWS) // TILE
    )
    keepm[...] = dot(dot_t(cols_in, tabk).astype(jnp.bfloat16), across)
    flag = jnp.broadcast_to(one_hot(branch_ref[...] > 0), (OUT, 15))
    branchm[...] = dot(flag, across)

    def multiply(n, t, step, begin=False):
        yy = (y + step + Y) % Y
        if t == 1 and n == 1 and step != 0:
            fourth = dot(block(1, yy, 0)[...], um[0])
            for g in (1, 2):
                fourth = fourth + dot(block(1, yy, g * PART)[...], um[g])
            block(1, yy, 3 * PART)[...] = fourth.astype(jnp.bfloat16)
        window = pl.multiple_of((yy % 2) * 1024, 1024)
        product = dot(lg[yy // 2, :, pl.ds(window, KWIN)], rb[t, yy])
        if begin:
            acc[t] = product
        else:
            acc[t] += product

    def scatter(t, run):
        for n in range(2):

            @pl.when(c == n)
            def _():
                i = t * 8
                for zd, low, rows, at in segments(2 * t + n):
                    for cd in range(2):
                        src = ct.at[t, cd, pl.ds(low, rows), :]
                        dst = zin.at[z, pl.ds(at, rows), :]
                        far = pltpu.make_async_remote_copy(
                            src_ref=src, dst_ref=dst, send_sem=zsend.at[i], recv_sem=zrecv.at[0],
                            device_id=(y * 2 + cd, x, jnp.int32(zd)), device_id_type=MESH,
                        )
                        if cd == n:

                            @pl.when(z != zd)
                            def _():
                                far.start() if run else far.wait_send()

                            if run:

                                @pl.when(z == zd)
                                def _():
                                    pltpu.make_async_copy(src, dst, zrecv.at[0]).start()
                        else:
                            far.start() if run else far.wait_send()
                        i += 1

    def turn(t):
        for cd in range(2):
            ct[t, cd] = acc[t, cd * TILE : cd * TILE + TILE, :].T

    points = (
        dict(
            la=(0, 2), o1=(0, 5), lb=(0, 7), o2=(0, 9), lf=(1, 3), m0a=(0, 12), m0b=(0, 13), m0c=(0, 13),
            m0d=(0, 13), m1a=(1, 8), m1b=(1, 9), m1c=(1, 10), m1d=(1, 11), end=(1, 13),
        ),
        dict(
            la=(0, 2), o1=(0, 5), lb=(0, 7), o2=(0, 9), lf=(1, 2), m0a=(0, 12), m0b=(0, 13), m0c=(0, 13),
            m0d=(1, 3), m1a=(1, 6), m1b=(1, 7), m1c=(1, 8), m1d=(1, 9), end=(1, 10),
        ),
    )

    def ring(n):
        at = points[n]
        pieces = {(d, t): hops(d, t, n) for d in ways for t in range(2)}
        order = [(0, k) for k in range(10)] + [(1, 0), (1, 1), (0, 10), (0, 11)]
        order += ([(1, 2), (1, 3)] if n == 0 else [(1, 2)]) + [(0, 12), (0, 13)]
        order += [(1, k) for k in (range(4, 14) if n == 0 else range(3, 11))]
        for t, k in order:
            for d in ways:
                mine_d = pieces[d, t]
                if k < len(mine_d):
                    hop, row = mine_d[k]
                    got(d, t, k, row, hop).wait()
                    if (hop + 1, row) in mine_d:
                        sent(d, t, mine_d.index((hop + 1, row)), row, hop + 1).start()
                if (t, k) == (0, 7):
                    for j in range(EARLY, 4 - n):
                        if n == 0:
                            first_hop(d, 1, j).start()
                        else:
                            sent(d, 1, j, *pieces[d, 1][j][::-1]).start()
            if (t, k) == at["la"]:
                for d in ways:
                    lgot(d, 0).wait()
                    lsent(d, 2).start()
                    lshare(d, 0).start()
            if (t, k) == at["o1"]:
                ogot(0, occx, X - 1)
                occy[y] = occx[0] + occx[1] + occx[2] + occx[3]
                for copy in stage_sends[1]:
                    copy.start()
            if (t, k) == at["lb"]:
                for d in ways:
                    lgot(d, 1).wait()
                    lshare(d, 1).start()
            if (t, k) == at["o2"]:
                ogot(1, occy, Y - 1)
                summed = occy[0]
                for j in range(1, Y):
                    summed = summed + occy[j]
                occc[c] = summed
                stage_sends[2][0].start()
            if (t, k) == at["lf"]:
                for d in ways:
                    lgot(d, 2).wait()
                    lshare(d, 2).start()
            if (t, k) == at["m0a"]:
                for d in ways:
                    for j in range(3):
                        lshared(d, j).wait()
                pltpu.make_async_copy(mine, mine, lsibr.at[6]).wait()
                for j in range(2 - n):
                    keep_own(j).wait()
                multiply(n, 0, 0, True)
                multiply(n, 0, 1)
                multiply(n, 0, -1)
                ogot(2, occc, 1)
                occz[z] = occc[0] + occc[1]
                agree(1, 2 * len(others), 1)
                for copy in stage_sends[3]:
                    copy.start()
            if (t, k) == at["m0b"]:
                multiply(n, 0, 2)
                multiply(n, 0, -2)
            if (t, k) == at["m0c"]:
                multiply(n, 0, 3)
                multiply(n, 0, -3)
            if (t, k) == at["m0d"]:
                multiply(n, 0, 4)
                turn(0)
                scatter(0, True)
            if (t, k) == at["m1a"]:
                multiply(n, 1, 0, True)
                multiply(n, 1, 1)
            if (t, k) == at["m1b"]:
                multiply(n, 1, -1)
                multiply(n, 1, 2)
            if (t, k) == at["m1c"]:
                multiply(n, 1, -2)
            if (t, k) == at["m1d"]:
                multiply(n, 1, 3)
                multiply(n, 1, -3)
            if (t, k) == at["end"]:
                multiply(n, 1, 4)
                turn(1)
                scatter(1, True)
        for (d, t), listed in pieces.items():
            for k, (hop, row) in enumerate(listed):
                sent(d, t, k, row, hop).wait_send()

    for n in range(2):

        @pl.when(c == n)
        def _():
            ring(n)

    ogot(3, occz, Z - 1)
    whole = occz[0]
    for j in range(1, Z):
        whole = whole + occz[j]
    mean = jnp.sum(whole, keepdims=True) / float(ROWS * 2 * Y)
    occ_ref[...] = jnp.broadcast_to(mean, (1, TILE))
    occ_store = pltpu.make_async_copy(occ_ref, occ_out, out_sem.at[0])
    occ_store.start()

    for d in ways:
        for k in range(3):
            lsent(d, k).wait_send()
            lshare(d, k).wait_send()
    for t in range(2):
        swap(t).wait_send()
    share_own.wait_send()
    for copies in stage_sends:
        for copy in copies:
            copy.wait_send()

    pltpu.make_async_copy(zin, zin, zrecv.at[0]).wait()
    square = zin[0]
    for j in range(1, Z):
        square = square + zin[j]
    square = square[:, :ROWS]
    doubled = 2.0 * win_ref[...].astype(jnp.float32) - square
    updated = jnp.where(branchm[...] > 0.5, doubled, square)
    out_ref[...] = jnp.where(keepm[...] > 0.5, updated, 0.0).astype(jnp.bfloat16)
    out_store = pltpu.make_async_copy(out_ref, out, out_sem.at[1])
    out_store.start()
    for t in range(2):
        scatter(t, False)
    occ_store.wait()
    out_store.wait()


def shards(row_stripe, column_stripe, window_block, stripe_tiles, column_tiles, keep_tiles, branch):
    bf, f32 = jnp.bfloat16, jnp.float32
    dma = pltpu.SemaphoreType.DMA
    block, occupancy = pl.pallas_call(
        kernel,
        out_shape=(
            jax.ShapeDtypeStruct((OUT, ROWS), bf),
            jax.ShapeDtypeStruct((1, TILE), f32),
        ),
        in_specs=[pl.BlockSpec(memory_space=pl.ANY)] * 7,
        out_specs=(pl.BlockSpec(memory_space=pl.ANY),) * 2,
        scratch_shapes=[
            pltpu.VMEM((ROWS, PANEL), bf),
            pltpu.VMEM((SUB, COLS), bf),
            pltpu.VMEM((OUT, ROWS), bf),
            pltpu.VMEM((15, 816), jnp.int32),
            pltpu.VMEM((15, 816), jnp.int32),
            pltpu.VMEM((15, 15), jnp.int32),
            pltpu.VMEM((1, 15), jnp.int32),
            dma((7,)),
            pltpu.VMEM((OUT, ROWS), bf),
            pltpu.VMEM((1, TILE), f32),
            dma((2,)),
            pltpu.VMEM((4, SUB, TILE), bf),
            pltpu.VMEM((2, Y, KWIN, TILE), bf),
            pltpu.VMEM((X, 2 * ROWS_P, PANEL), bf),
            pltpu.VMEM((2, 2 * ROWS_P, TILE), f32),
            pltpu.VMEM((2, 2, TILE, TILE), f32),
            pltpu.VMEM((Z, OUT, TILE), f32),
            pltpu.VMEM((X, 8, TILE), f32),
            pltpu.VMEM((Y, 8, TILE), f32),
            pltpu.VMEM((2, 8, TILE), f32),
            pltpu.VMEM((Z, 8, TILE), f32),
            pltpu.VMEM((OUT, ROWS), f32),
            pltpu.VMEM((OUT, ROWS), f32),
            pltpu.VMEM((3, TILE, TILE), bf),
            dma((4 * STEPS,)), dma((4 * STEPS,)), pltpu.SemaphoreType.REGULAR((2,)),
            dma((2,)), dma((2,)), dma((2,)),
            dma((6,)), dma((6,)), dma((7,)), dma((7,)),
            dma((16,)), dma((1,)),
            dma((22,)), dma((4,)),
        ],
        compiler_params=pltpu.CompilerParams(
            collective_id=0, has_side_effects=True, vmem_limit_bytes=56 * 2**20
        ),
        name="square",
    )(
        row_stripe[:, 0, :], column_stripe[0], window_block.T, stripe_tiles, column_tiles.T,
        keep_tiles, branch[None, :],
    )
    return block.T, occupancy[0, 0]


def solution(mesh):
    return jax.shard_map(
        shards,
        mesh=mesh,
        in_specs=(
            P("row", "depth", "col"),
            P("depth", "row", "col"),
            P("row", ("col", "depth")),
            P(),
            P(),
            P(),
            P(),
        ),
        out_specs=(P("row", ("col", "depth")), P()),
        check_vma=False,
    )
```

```python
import functools

import jax
import jax.numpy as jnp
from jax import lax
from jax.experimental import pallas as pl
from jax.experimental.pallas import tpu as pltpu
from jax.sharding import PartitionSpec as P

TILE = 128
MESH = pl.DeviceIdType.MESH
X, Y, Z = 4, 8, 12
ROWS = 120
ROWS_P = 128
PANEL = 2176
SUB = 544
COLS = 480
OUT = 40
KWIN = 1152
PART = 272
EARLY = 2
STEPS = 14
LAST = COLS - 3 * TILE
SPARE = TILE - LAST


def segments(tile):
    found = []
    for z in range(Z):
        low = max(tile * TILE, z * OUT)
        high = min(tile * TILE + TILE, COLS, z * OUT + OUT)
        if low < high:
            found.append((z, low - tile * TILE, high - low, low - z * OUT))
    return found


def hops(d, t, core):
    if t == 1 and core == 1:
        first = [2 * PART, 0, PART]
        third = first if d > 0 else [PART, 2 * PART, 0]
        fourth = first[:2] if d > 0 else [PART]
    else:
        own = [core * SUB, core * SUB + PART]
        other = [SUB - core * SUB, SUB - core * SUB + PART]
        first = own + other
        third = first if d > 0 else other + own
        fourth = own if d > 0 else other
    return [(h + 1, row) for h, rows in enumerate((first, first, third, fourth)) for row in rows]


def one_hot(hit):
    return jnp.where(hit, 1.0, 0.0).astype(jnp.bfloat16)


def dot(a, b):
    return jnp.dot(a, b, preferred_element_type=jnp.float32)


def dot_t(a, b):
    dims = (((1,), (1,)), ((), ()))
    return lax.dot_general(a, b, dims, preferred_element_type=jnp.float32)


def kernel(
    row_in, col_in, win_in, stripe_in, ctab_in, keep_in, branch_in,
    out, occ_out,
    row_ref, col_ref, win_ref, stripe_ref, ctab_ref, keep_ref, branch_ref, in_sem, out_ref, occ_ref, out_sem,
    rm, rb, lg, acc, ct, zin, occx, occy, occc, occz, keepm, branchm, um,
    rsend, rrecv, go, dsend, drecv, own_sem, lsend, lrecv, lsibs, lsibr, zsend, zrecv, osend, orecv,
):
    r = lax.axis_index("row")
    x = lax.axis_index("col")
    z = lax.axis_index("depth")
    y = r // 2
    c = r % 2

    def ydev(d):
        return (((y + d) % Y) * 2 + c, x, z)

    def xdev(d):
        return (r, (x + d) % X, z)

    sib = (y * 2 + (1 - c), x, z)

    arrays = [
        (ctab_in, ctab_ref), (col_in, col_ref), (stripe_in, stripe_ref), (row_in, row_ref),
        (keep_in, keep_ref), (branch_in, branch_ref), (win_in, win_ref),
    ]
    loads = [pltpu.make_async_copy(a, b, in_sem.at[i]) for i, (a, b) in enumerate(arrays)]
    barrier = pltpu.get_barrier_semaphore()
    plane = [((y + d) % Y * 2, x, z) for d in range(1, Y)] + [(y * 2, (x + d) % X, z) for d in range(1, X)]
    others = [(y * 2 + 1, x, (z + d) % Z) for d in range(1, Z)]
    for peer in plane:
        pl.semaphore_signal(barrier, inc=1, device_id=peer, device_id_type=MESH)

    @pl.when(c == 1)
    def _():
        pl.semaphore_signal(barrier, inc=1, device_id=sib, device_id_type=MESH)

    for load in loads:
        load.start()

    def agree(counter, count, i):
        @pl.when(c == counter)
        def _():
            pl.semaphore_wait(barrier, count)
            pl.semaphore_signal(go.at[i], inc=1, device_id=sib, device_id_type=MESH)

        @pl.when(c != counter)
        def _():
            pl.semaphore_wait(go.at[i], 1)

    for t in range(2):
        for yy in range(Y):
            low = 0 if yy % 2 else 2 * SUB
            rb[t, yy, low : low + 64, :] = jnp.zeros((64, TILE), jnp.bfloat16)

    first = z * 68 + (r * SUB) // TILE
    skew = (r * SUB) % TILE
    loads[0].wait()
    ctab = one_hot(ctab_ref[...] > 0)
    pick = one_hot(
        lax.broadcasted_iota(jnp.int32, (16, 816), 1)
        == lax.broadcasted_iota(jnp.int32, (16, 816), 0) + first
    )
    picked = dot_t(pick, ctab).astype(jnp.bfloat16)
    spread = one_hot(
        lax.broadcasted_iota(jnp.int32, (15, 512), 0)
        == (lax.broadcasted_iota(jnp.int32, (15, 512), 1) + x * COLS) // TILE
    )
    by_col = dot(picked, spread).astype(jnp.bfloat16)
    band = one_hot(
        lax.broadcasted_iota(jnp.int32, (SUB, 16), 1)
        == (lax.broadcasted_iota(jnp.int32, (SUB, 16), 0) + skew) // TILE
    )

    def masked(tile):
        wide = min(TILE, COLS - tile * TILE)
        if wide < TILE:
            rm[tile] = jnp.zeros((SUB, TILE), jnp.bfloat16)
        mask = dot(band, by_col[:, tile * TILE : tile * TILE + wide]).astype(jnp.bfloat16)
        rm[tile, :, 0:wide] = col_ref[:, tile * TILE : tile * TILE + wide] * mask

    loads[1].wait()
    for n in range(2):

        @pl.when(c == n)
        def _():
            masked(n)

    agree(0, 2 * len(plane) + 1, 0)

    def off(yy, cc):
        return pl.multiple_of((yy % 2) * 64 + cc * SUB, 32)

    def piece(t, yy, cc):
        return rb.at[t, yy, pl.ds(off(yy, cc), SUB), :]

    def block(t, yy, row):
        start = pl.multiple_of((yy % 2) * 64 + row, 16)
        return rb.at[t, yy, pl.ds(start, PART), :]

    def sent(d, t, k, row, hop, here=None):
        there = block(t, (y - d * (hop - 1) + Y) % Y, row)
        i = ((0 if d > 0 else 2) + t) * STEPS + k
        return pltpu.make_async_remote_copy(
            src_ref=there if here is None else here, dst_ref=there, send_sem=rsend.at[i],
            recv_sem=rrecv.at[i], device_id=ydev(d % Y), device_id_type=MESH,
        )

    def got(d, t, k, row, hop):
        here = block(t, (y - d * hop + Y) % Y, row)
        i = ((0 if d > 0 else 2) + t) * STEPS + k
        return pltpu.make_async_copy(here, here, rrecv.at[i])

    def first_hop(d, t, k):
        part = (k % 2) * PART
        if k < 2:
            return sent(d, t, k, c * SUB + part, 1, rm.at[2 * t + c, part : part + PART, :])
        return sent(d, t, k, (1 - c) * SUB + part, 1)

    ways = (1, -1)
    for k in range(2):
        for d in ways:
            first_hop(d, 0, k).start()

    def swap(t):
        return pltpu.make_async_remote_copy(
            src_ref=rm.at[2 * t + 1 - c], dst_ref=piece(t, y, c),
            send_sem=dsend.at[t], recv_sem=drecv.at[t], device_id=sib, device_id_type=MESH,
        )

    def keep_own(t):
        return pltpu.make_async_copy(rm.at[2 * t + c], piece(t, y, c), own_sem.at[t])

    def swapped(t):
        here = piece(t, y, 1 - c)
        return pltpu.make_async_copy(here, here, drecv.at[t])

    for n in range(2):

        @pl.when(c != n)
        def _():
            masked(n)

    swap(0).start()
    keep_own(0).start()
    for peer in others:
        pl.semaphore_signal(barrier, inc=1, device_id=peer, device_id_type=MESH)
    masked(2)
    masked(3)
    swap(1).start()

    @pl.when(c == 0)
    def _():
        keep_own(1).start()


    loads[2].wait()
    loads[3].wait()
    stab = one_hot(stripe_ref[...] > 0)
    base = z * 68 + x * 17
    shift = one_hot(
        lax.broadcasted_iota(jnp.int32, (816, TILE), 0)
        == lax.broadcasted_iota(jnp.int32, (816, TILE), 1) + base
    )
    narrow = dot(stab, shift).astype(jnp.bfloat16)
    rows_in = one_hot(
        lax.broadcasted_iota(jnp.int32, (ROWS, 15), 1)
        == (lax.broadcasted_iota(jnp.int32, (ROWS, 15), 0) + r * ROWS) // TILE
    )
    lmask = dot(rows_in, narrow)
    total = jnp.zeros((8, TILE), jnp.float32)
    myrow = pl.multiple_of(c * ROWS_P, ROWS_P)
    for k in range(17):
        part = row_ref[:, k * TILE : k * TILE + TILE].astype(jnp.float32)
        part = part * lmask[:, k : k + 1]
        total = total + jnp.sum((part * part).reshape(15, 8, TILE), axis=0)
        whole = jnp.concatenate([part, jnp.zeros((8, TILE), jnp.float32)], axis=0)
        lg[x, pl.ds(myrow, ROWS_P), k * TILE : k * TILE + TILE] = whole.astype(jnp.bfloat16)
    occx[x] = total

    def half(panel, low):
        return lg.at[panel, pl.ds(pl.multiple_of(myrow + low, 64), 64), :]

    def lowrow(d, k):
        ahead = 0 if d > 0 else 64
        return 64 - ahead if k == 1 else ahead

    def lindex(d, k):
        return (0 if d > 0 else 3) + k

    def lsent(d, k):
        panel = (x - d + X) % X if k == 2 else x
        ref = half(panel, lowrow(d, k))
        return pltpu.make_async_remote_copy(
            src_ref=ref, dst_ref=ref, send_sem=lsend.at[lindex(d, k)],
            recv_sem=lrecv.at[lindex(d, k)], device_id=xdev(d % X), device_id_type=MESH,
        )

    def lpart(d, k):
        panel = (x - (2 * d if k == 2 else d) + X) % X
        return half(panel, lowrow(d, k))

    def lgot(d, k):
        here = lpart(d, k)
        return pltpu.make_async_copy(here, here, lrecv.at[lindex(d, k)])

    def lshare(d, k):
        ref = lpart(d, k)
        return pltpu.make_async_remote_copy(
            src_ref=ref, dst_ref=ref, send_sem=lsibs.at[lindex(d, k)],
            recv_sem=lsibr.at[lindex(d, k)], device_id=sib, device_id_type=MESH,
        )

    otherrow = pl.multiple_of((1 - c) * ROWS_P, ROWS_P)

    def lshared(d, k):
        panel = (x - (2 * d if k == 2 else d) + X) % X
        here = lg.at[panel, pl.ds(pl.multiple_of(otherrow + lowrow(d, k), 64), 64), :]
        return pltpu.make_async_copy(here, here, lsibr.at[lindex(d, k)])

    mine = lg.at[x, pl.ds(myrow, ROWS_P), :]
    share_own = pltpu.make_async_remote_copy(
        src_ref=mine, dst_ref=mine, send_sem=lsibs.at[6], recv_sem=lsibr.at[6],
        device_id=sib, device_id_type=MESH,
    )

    for k in range(2):
        for d in ways:
            lsent(d, k).start()
    share_own.start()

    swapped(0).wait()
    for k in range(2, 4):
        for d in ways:
            first_hop(d, 0, k).start()

    lane_in = lax.broadcasted_iota(jnp.int32, (TILE, TILE), 0)
    lane_out = lax.broadcasted_iota(jnp.int32, (TILE, TILE), 1)
    for g in range(3):
        um[g] = one_hot((lane_in >= LAST) & (lane_in - LAST + g * SPARE == lane_out))

    swapped(1).wait()

    @pl.when(c == 0)
    def _():
        for k in range(EARLY):
            for d in ways:
                first_hop(d, 1, k).start()

    @pl.when(c == 1)
    def _():
        fourth = rm[3, PART:SUB, :]
        block(1, y, 3 * PART)[...] = fourth
        for g in (2, 0, 1):
            main = rm[3, 0:PART, :] if g == 2 else block(1, y, g * PART)[...]
            extra = dot_t(fourth, um[g])
            block(1, y, g * PART)[...] = (main.astype(jnp.float32) + extra).astype(jnp.bfloat16)
        for k in range(min(EARLY, 3)):
            for d in ways:
                sent(d, 1, k, *hops(d, 1, 1)[k][::-1]).start()

    def osent(stage, i, buf, slot, device):
        return pltpu.make_async_remote_copy(
            src_ref=buf.at[slot], dst_ref=buf.at[slot], send_sem=osend.at[i],
            recv_sem=orecv.at[stage], device_id=device, device_id_type=MESH,
        )

    stage_sends = [
        [osent(0, d - 1, occx, x, xdev(d)) for d in range(1, X)],
        [osent(1, 2 + d, occy, y, ydev(d)) for d in range(1, Y)],
        [osent(2, 10, occc, c, sib)],
        [osent(3, 10 + d, occz, z, (r, x, (z + d) % Z)) for d in range(1, Z)],
    ]

    def ogot(stage, buf, n):
        here = buf.at[pl.ds(0, n)]
        pltpu.make_async_copy(here, here, orecv.at[stage]).wait()

    for copy in stage_sends[0]:
        copy.start()

    for load in loads[4:]:
        load.wait()
    tabk = one_hot(keep_ref[...] > 0)
    cols_in = one_hot(
        lax.broadcasted_iota(jnp.int32, (OUT, 15), 1)
        == (lax.broadcasted_iota(jnp.int32, (OUT, 15), 0) + x * COLS + z * OUT) // TILE
    )
    across = one_hot(
        lax.broadcasted_iota(jnp.int32, (15, ROWS), 0)
        == (lax.broadcasted_iota(jnp.int32, (15, ROWS), 1) + r * ROWS) // TILE
    )
    keepm[...] = dot(dot_t(cols_in, tabk).astype(jnp.bfloat16), across)
    flag = jnp.broadcast_to(one_hot(branch_ref[...] > 0), (OUT, 15))
    branchm[...] = dot(flag, across)

    def multiply(n, t, step, begin=False):
        yy = (y + step + Y) % Y
        if t == 1 and n == 1 and step != 0:
            fourth = dot(block(1, yy, 0)[...], um[0])
            for g in (1, 2):
                fourth = fourth + dot(block(1, yy, g * PART)[...], um[g])
            block(1, yy, 3 * PART)[...] = fourth.astype(jnp.bfloat16)
        window = pl.multiple_of((yy % 2) * 1024, 1024)
        product = dot(lg[yy // 2, :, pl.ds(window, KWIN)], rb[t, yy])
        if begin:
            acc[t] = product
        else:
            acc[t] += product

    def scatter(t, run):
        for n in range(2):

            @pl.when(c == n)
            def _():
                i = t * 8
                for zd, low, rows, at in segments(2 * t + n):
                    for cd in range(2):
                        src = ct.at[t, cd, pl.ds(low, rows), :]
                        dst = zin.at[z, pl.ds(at, rows), :]
                        far = pltpu.make_async_remote_copy(
                            src_ref=src, dst_ref=dst, send_sem=zsend.at[i], recv_sem=zrecv.at[0],
                            device_id=(y * 2 + cd, x, jnp.int32(zd)), device_id_type=MESH,
                        )
                        if cd == n:

                            @pl.when(z != zd)
                            def _():
                                far.start() if run else far.wait_send()

                            if run:

                                @pl.when(z == zd)
                                def _():
                                    pltpu.make_async_copy(src, dst, zrecv.at[0]).start()
                        else:
                            far.start() if run else far.wait_send()
                        i += 1

    def turn(t):
        for cd in range(2):
            ct[t, cd] = acc[t, cd * TILE : cd * TILE + TILE, :].T

    points = (
        dict(
            la=(0, 2), o1=(0, 5), lb=(0, 7), o2=(0, 9), lf=(1, 3), m0a=(0, 12), m0b=(0, 13), m0c=(0, 13),
            m0d=(0, 13), m1a=(1, 8), m1b=(1, 9), m1c=(1, 10), m1d=(1, 11), end=(1, 13),
        ),
        dict(
            la=(0, 2), o1=(0, 5), lb=(0, 7), o2=(0, 9), lf=(1, 2), m0a=(0, 12), m0b=(0, 13), m0c=(0, 13),
            m0d=(1, 3), m1a=(1, 6), m1b=(1, 7), m1c=(1, 8), m1d=(1, 9), end=(1, 10),
        ),
    )

    def ring(n):
        at = points[n]
        pieces = {(d, t): hops(d, t, n) for d in ways for t in range(2)}
        order = [(0, k) for k in range(10)] + [(1, 0), (1, 1), (0, 10), (0, 11)]
        order += ([(1, 2), (1, 3)] if n == 0 else [(1, 2)]) + [(0, 12), (0, 13)]
        order += [(1, k) for k in (range(4, 14) if n == 0 else range(3, 11))]
        for t, k in order:
            for d in ways:
                mine_d = pieces[d, t]
                if k < len(mine_d):
                    hop, row = mine_d[k]
                    got(d, t, k, row, hop).wait()
                    if (hop + 1, row) in mine_d:
                        sent(d, t, mine_d.index((hop + 1, row)), row, hop + 1).start()
                if (t, k) == (0, 7):
                    for j in range(EARLY, 4 - n):
                        if n == 0:
                            first_hop(d, 1, j).start()
                        else:
                            sent(d, 1, j, *pieces[d, 1][j][::-1]).start()
            if (t, k) == at["la"]:
                for d in ways:
                    lgot(d, 0).wait()
                    lsent(d, 2).start()
                    lshare(d, 0).start()
            if (t, k) == at["o1"]:
                ogot(0, occx, X - 1)
                occy[y] = occx[0] + occx[1] + occx[2] + occx[3]
                for copy in stage_sends[1]:
                    copy.start()
            if (t, k) == at["lb"]:
                for d in ways:
                    lgot(d, 1).wait()
                    lshare(d, 1).start()
            if (t, k) == at["o2"]:
                ogot(1, occy, Y - 1)
                summed = occy[0]
                for j in range(1, Y):
                    summed = summed + occy[j]
                occc[c] = summed
                stage_sends[2][0].start()
            if (t, k) == at["lf"]:
                for d in ways:
                    lgot(d, 2).wait()
                    lshare(d, 2).start()
            if (t, k) == at["m0a"]:
                for d in ways:
                    for j in range(3):
                        lshared(d, j).wait()
                pltpu.make_async_copy(mine, mine, lsibr.at[6]).wait()
                for j in range(2 - n):
                    keep_own(j).wait()
                multiply(n, 0, 0, True)
                multiply(n, 0, 1)
                multiply(n, 0, -1)
                ogot(2, occc, 1)
                occz[z] = occc[0] + occc[1]
                agree(1, 2 * len(others), 1)
                for copy in stage_sends[3]:
                    copy.start()
            if (t, k) == at["m0b"]:
                multiply(n, 0, 2)
                multiply(n, 0, -2)
            if (t, k) == at["m0c"]:
                multiply(n, 0, 3)
                multiply(n, 0, -3)
            if (t, k) == at["m0d"]:
                multiply(n, 0, 4)
                turn(0)
                scatter(0, True)
            if (t, k) == at["m1a"]:
                multiply(n, 1, 0, True)
                multiply(n, 1, 1)
            if (t, k) == at["m1b"]:
                multiply(n, 1, -1)
                multiply(n, 1, 2)
            if (t, k) == at["m1c"]:
                multiply(n, 1, -2)
            if (t, k) == at["m1d"]:
                multiply(n, 1, 3)
                multiply(n, 1, -3)
            if (t, k) == at["end"]:
                multiply(n, 1, 4)
                turn(1)
                scatter(1, True)
        for (d, t), listed in pieces.items():
            for k, (hop, row) in enumerate(listed):
                sent(d, t, k, row, hop).wait_send()

    for n in range(2):

        @pl.when(c == n)
        def _():
            ring(n)

    ogot(3, occz, Z - 1)
    whole = occz[0]
    for j in range(1, Z):
        whole = whole + occz[j]
    mean = jnp.sum(whole, keepdims=True) / float(ROWS * 2 * Y)
    occ_ref[...] = jnp.broadcast_to(mean, (1, TILE))
    occ_store = pltpu.make_async_copy(occ_ref, occ_out, out_sem.at[0])
    occ_store.start()

    for d in ways:
        for k in range(3):
            lsent(d, k).wait_send()
            lshare(d, k).wait_send()
    for t in range(2):
        swap(t).wait_send()
    share_own.wait_send()
    for copies in stage_sends:
        for copy in copies:
            copy.wait_send()

    pltpu.make_async_copy(zin, zin, zrecv.at[0]).wait()
    square = zin[0]
    for j in range(1, Z):
        square = square + zin[j]
    square = square[:, :ROWS]
    doubled = 2.0 * win_ref[...].astype(jnp.float32) - square
    updated = jnp.where(branchm[...] > 0.5, doubled, square)
    out_ref[...] = jnp.where(keepm[...] > 0.5, updated, 0.0).astype(jnp.bfloat16)
    out_store = pltpu.make_async_copy(out_ref, out, out_sem.at[1])
    out_store.start()
    for t in range(2):
        scatter(t, False)
    occ_store.wait()
    out_store.wait()


def shards(row_stripe, column_stripe, window_block, stripe_tiles, column_tiles, keep_tiles, branch):
    bf, f32 = jnp.bfloat16, jnp.float32
    dma = pltpu.SemaphoreType.DMA
    block, occupancy = pl.pallas_call(
        kernel,
        out_shape=(
            jax.ShapeDtypeStruct((OUT, ROWS), bf),
            jax.ShapeDtypeStruct((1, TILE), f32),
        ),
        in_specs=[pl.BlockSpec(memory_space=pl.ANY)] * 7,
        out_specs=(pl.BlockSpec(memory_space=pl.ANY),) * 2,
        scratch_shapes=[
            pltpu.VMEM((ROWS, PANEL), bf),
            pltpu.VMEM((SUB, COLS), bf),
            pltpu.VMEM((OUT, ROWS), bf),
            pltpu.VMEM((15, 816), jnp.int32),
            pltpu.VMEM((15, 816), jnp.int32),
            pltpu.VMEM((15, 15), jnp.int32),
            pltpu.VMEM((1, 15), jnp.int32),
            dma((7,)),
            pltpu.VMEM((OUT, ROWS), bf),
            pltpu.VMEM((1, TILE), f32),
            dma((2,)),
            pltpu.VMEM((4, SUB, TILE), bf),
            pltpu.VMEM((2, Y, KWIN, TILE), bf),
            pltpu.VMEM((X, 2 * ROWS_P, PANEL), bf),
            pltpu.VMEM((2, 2 * ROWS_P, TILE), f32),
            pltpu.VMEM((2, 2, TILE, TILE), f32),
            pltpu.VMEM((Z, OUT, TILE), f32),
            pltpu.VMEM((X, 8, TILE), f32),
            pltpu.VMEM((Y, 8, TILE), f32),
            pltpu.VMEM((2, 8, TILE), f32),
            pltpu.VMEM((Z, 8, TILE), f32),
            pltpu.VMEM((OUT, ROWS), f32),
            pltpu.VMEM((OUT, ROWS), f32),
            pltpu.VMEM((3, TILE, TILE), bf),
            dma((4 * STEPS,)), dma((4 * STEPS,)), pltpu.SemaphoreType.REGULAR((2,)),
            dma((2,)), dma((2,)), dma((2,)),
            dma((6,)), dma((6,)), dma((7,)), dma((7,)),
            dma((16,)), dma((1,)),
            dma((22,)), dma((4,)),
        ],
        compiler_params=pltpu.CompilerParams(
            collective_id=0, has_side_effects=True, vmem_limit_bytes=56 * 2**20
        ),
        name="square",
    )(
        row_stripe[:, 0, :], column_stripe[0], window_block.T, stripe_tiles, column_tiles.T,
        keep_tiles, branch[None, :],
    )
    return block.T, occupancy[0, 0]


def solution(mesh):
    return jax.shard_map(
        shards,
        mesh=mesh,
        in_specs=(
            P("row", "depth", "col"),
            P("depth", "row", "col"),
            P("row", ("col", "depth")),
            P(),
            P(),
            P(),
            P(),
        ),
        out_specs=(P("row", ("col", "depth")), P()),
        check_vma=False,
    )
```
